256 devices in a mesh: gx: 16 (over y_lo, z), gy: 16 (over x, y_hi, core).
Axes of the slice: x: 4, y: 4 (y_hi: 2, y_lo: 2; y = y_hi * 2 + y_lo), z: 8, core: 2. Of those that a mesh axis runs over, the one named last changes fastest.
Arguments:
- density: float32 [2, 256, 2048], P(None, 'gx', 'gy'), may hold values from 0.5 to 2
- momentum: float32 [3, 2, 256, 2048], P(None, None, 'gx', 'gy'), may hold values from -1.2 to 1.2
- field: float32 [3, 2, 256, 2048], P(None, None, 'gx', 'gy'), may hold values from -2 to 2
- fargo_offsets: int32 [2, 256], P(None, 'gx'), may hold values from 0 to 2047
- shear_shift: int32 [2], replicated, may hold values from 0 to 2047
Outputs:
- new_density: float32 [2, 256, 2048], P(None, 'gx', 'gy')
- new_momentum: float32 [3, 2, 256, 2048], P(None, None, 'gx', 'gy')
- new_field: float32 [3, 2, 256, 2048], P(None, None, 'gx', 'gy')
The draws below stay inside these ranges and needn't reach their ends.
Inputs may be any that keep to these rules, and one draw needn't show every extreme that they name: `fargo_offsets`: column offsets are cell counts along the azimuth. `shear_shift`: the shift is held fixed within a step.
All inputs are finite; a program needn't handle non-finite values.
Results may differ from the reference program's by a relative error of at most 0.00002.
Values sent between devices are 32-bit elements; how exact they have to be, the bound alone decides.
No kernel may reach another device: no remote copies, remote signals or barrier semaphores. Data moves between devices by JAX's collectives and lax.ppermute only.
A program may use at most 64 MiB of HBM per device.

```python
import math
import jax
import jax.numpy as jnp

CZ = 2
STEPS = 2
NX = 256
NY = 2048


def touch_ends(array, key, least, largest):
    shape = array.shape
    place = [jax.random.randint(jax.random.fold_in(key, axis), (), 0, shape[axis]) for axis in range(len(shape))]
    array = array.at[tuple(place)].set(least)
    longest = shape.index(max(shape))
    place[longest] = (place[longest] + 1) % shape[longest]
    return array.at[tuple(place)].set(largest)


def block_scale(rng, shape, shards, least, top_value):
    gain, own = 1.0, jax.random.fold_in(rng, 6)
    for dim, shards_of in shards:
        draws = jnp.exp(jax.random.uniform(jax.random.fold_in(own, dim), (shards_of,), jnp.float32, least / len(shards), top_value / len(shards)))
        gain = gain * jnp.repeat(draws, shape[dim] // shards_of).reshape([-1 if axis == dim else 1 for axis in range(len(shape))])
    return gain


def scatter_about(own_key, extent, scale, reach, pieces=(), dtype=jnp.bfloat16):
    array = scale * jax.random.normal(own_key, extent, jnp.float32)
    if pieces:
        array = array * block_scale(own_key, extent, pieces, -0.22, 0.18)
    return jnp.clip(array, -reach, reach).astype(dtype)


def setup_inputs(seed: int = 0) -> dict:
    streams_of = jax.random.split(jax.random.key(seed), 6)
    return {
        "density": jnp.clip(jnp.exp(math.log(2.0) - 1.3862944 * jax.random.uniform(streams_of[0], (CZ, NX, NY), jnp.float32) ** block_scale(streams_of[0], (CZ, NX, NY), ((1, 16), (2, 16)), -0.2, 0.2)), 0.5, 2.0),
        "momentum": scatter_about(streams_of[1], (3, CZ, NX, NY), 0.3, 1.2, ((2, 16), (3, 16)), jnp.float32),
        "field": scatter_about(streams_of[2], (3, CZ, NX, NY), 0.5, 2.0, ((2, 16), (3, 16)), jnp.float32),
        "fargo_offsets": touch_ends(jax.random.randint(streams_of[3], (STEPS, NX), 0, NY), jax.random.fold_in(streams_of[3], 1), 0, NY - 1).astype(jnp.int32),
        "shear_shift": jax.random.randint(streams_of[4], (STEPS,), 0, NY).astype(jnp.int32),
    }


time_step = 0.03
rotation = 1.0
shear_rate = 1.5
sound_square = 1.0

def ahead(values, axis):
    return jnp.roll(values, -1, axis)

def behind(values, axis):
    return jnp.roll(values, 1, axis)

def wave_pieces(state, normal):
    density, along, across_one, across_two, field_one, field_two = state
    pressure = sound_square * density + 0.5 * (field_one * field_one + field_two * field_two - normal * normal)
    conserved = (density, density * along, density * across_one, density * across_two, field_one, field_two)
    fluxes = (density * along, density * along * along + pressure, density * along * across_one - normal * field_one, density * along * across_two - normal * field_two, field_one * along - normal * across_one, field_two * along - normal * across_two)
    signal = jnp.sqrt(sound_square + (normal * normal + field_one * field_one + field_two * field_two) / density)
    return (conserved, fluxes, along - signal, along + signal)

def interface_flux(left_state, right_state, normal):
    cons_left, flux_left, low_left, high_left = wave_pieces(left_state, normal)
    cons_right, flux_right, low_right, high_right = wave_pieces(right_state, normal)
    lowest = jnp.minimum(jnp.minimum(low_left, low_right), 0.0)
    highest = jnp.maximum(jnp.maximum(high_left, high_right), 0.0)
    inverse = 1.0 / (highest - lowest)
    return tuple(((highest * one_flux - lowest * two_flux + lowest * highest * (two_cons - one_cons)) * inverse for one_cons, two_cons, one_flux, two_flux in zip(cons_left, cons_right, flux_left, flux_right)))

def shifted(values, axis):
    return tuple((ahead(member, axis) for member in values))

def diverge(along_x, along_y, along_z):
    return along_x - behind(along_x, 1) + (along_y - behind(along_y, 2)) + (along_z - behind(along_z, 0))

def tendency(state):
    density = state[0]
    velocity_x = state[1] / density
    velocity_y = state[2] / density
    velocity_z = state[3] / density
    field_x, field_y, field_z = (state[4], state[5], state[6])
    center_x = 0.5 * (field_x + behind(field_x, 1))
    center_y = 0.5 * (field_y + behind(field_y, 2))
    center_z = 0.5 * (field_z + behind(field_z, 0))
    cells_x = (density, velocity_x, velocity_y, velocity_z, center_y, center_z)
    cells_y = (density, velocity_y, velocity_z, velocity_x, center_z, center_x)
    cells_z = (density, velocity_z, velocity_x, velocity_y, center_x, center_y)
    flux_x = interface_flux(cells_x, shifted(cells_x, 1), field_x)
    flux_y = interface_flux(cells_y, shifted(cells_y, 2), field_y)
    flux_z = interface_flux(cells_z, shifted(cells_z, 0), field_z)
    edge_z = 0.25 * (-flux_x[4] - ahead(flux_x[4], 2) + flux_y[5] + ahead(flux_y[5], 1))
    edge_x = 0.25 * (-flux_y[4] - ahead(flux_y[4], 0) + flux_z[5] + ahead(flux_z[5], 2))
    edge_y = 0.25 * (flux_x[5] + ahead(flux_x[5], 0) - flux_z[4] - ahead(flux_z[4], 1))
    rate_density = -diverge(flux_x[0], flux_y[0], flux_z[0])
    rate_radial = -diverge(flux_x[1], flux_y[3], flux_z[2]) + 2.0 * rotation * state[2]
    rate_azimuth = -diverge(flux_x[2], flux_y[1], flux_z[3]) - (2.0 - shear_rate) * rotation * state[1]
    rate_vertical = -diverge(flux_x[3], flux_y[2], flux_z[1])
    rate_fx = -(edge_z - behind(edge_z, 2) - (edge_y - behind(edge_y, 0)))
    rate_fy = -(edge_x - behind(edge_x, 0) - (edge_z - behind(edge_z, 1)))
    rate_fz = -(edge_y - behind(edge_y, 1) - (edge_x - behind(edge_x, 2)))
    return time_step * jnp.stack([rate_density, rate_radial, rate_azimuth, rate_vertical, rate_fx, rate_fy, rate_fz])

def extend(state, shift, width):
    lower = jnp.roll(state[:, :, NX - width:, :], -shift, axis=3)
    upper = jnp.roll(state[:, :, :width, :], shift, axis=3)
    extended = jnp.concatenate([lower, state, upper], axis=2)
    return jnp.concatenate([extended[..., NY - width:], extended, extended[..., :width]], axis=3)

def crop_margin(values, width):
    return values[:, :, width:-width, width:-width]

def remap_columns(state, offsets):
    return jax.vmap(lambda column, amount: jnp.roll(column, amount, axis=-1), in_axes=(2, 0), out_axes=2)(state, offsets)

def reference(density, momentum, field, fargo_offsets, shear_shift):
    state = jnp.concatenate([density[None], momentum, field], axis=0)
    for level in range(STEPS):
        shift = shear_shift[level]
        padded = extend(state, shift, 2)
        first = crop_margin(padded + tendency(padded), 2)
        padded = extend(first, shift, 2)
        updated = 0.5 * state + 0.5 * crop_margin(padded + tendency(padded), 2)
        state = remap_columns(updated, fargo_offsets[level])
    return (state[0], state[1:4], state[4:7])
```

```python
import functools

import jax
import jax.numpy as jnp
from jax import lax
from jax.experimental import pallas as pl
from jax.experimental.pallas import tpu as pltpu
from jax.sharding import PartitionSpec as P

time_step = 0.03
rotation = 1.0
shear_rate = 1.5

ROWS = 16
LANES = 128
PARTS = 16
LEVELS = 2
SLABS = 14
BELOW = 5
ABOVE = 4
FULL = 9
LOW_ROWS = 72
UP_ROWS = 64


def slab(density, momentum, field, index):
    member, level = divmod(index, 2)
    if member == 0:
        return density[level]
    if member < 4:
        return momentum[member - 1, level]
    return field[member - 4, level]


def strip_kernel(density, momentum, field, offsets, low, up):
    low[...] = jnp.zeros_like(low)
    up[...] = jnp.zeros_like(up)
    for index in range(SLABS):
        rows = slab(density, momentum, field, index)
        low[pl.ds(index, BELOW, stride=SLABS), :] = rows[ROWS - BELOW :]
        up[pl.ds(index, ABOVE, stride=SLABS), :] = rows[:ABOVE]
    shifts = offsets[...].astype(jnp.float32)
    low[70:72, 0:ROWS] = shifts
    up[56:58, 0:ROWS] = shifts


def pack_kernel(density, momentum, field, low, up, send, ghost_offsets, rows_of):
    rows_of[0:70, :] = low[0:70, :]
    for index in range(SLABS):
        rows_of[pl.ds(BELOW * SLABS + index, ROWS, stride=SLABS), :] = slab(
            density, momentum, field, index
        )
    rows_of[294:350, :] = up[0:56, :]
    for part in range(PARTS):
        start = SLABS * (part + 1)
        send[part, 0:126, :] = rows_of[start : start + 126, :]
        start = SLABS * part + 8
        send[part, 126:128, :] = rows_of[start : start + 2, :]
    ghost_offsets[0:2, :] = low[70:72, :].astype(jnp.int32)
    ghost_offsets[2:4, :] = up[56:58, :].astype(jnp.int32)


def y_ahead(values, lane, sublane):
    turned = pltpu.roll(values, LANES - 1, 1)
    return jnp.where(lane == LANES - 1, pltpu.roll(turned, ROWS - 1, 0), turned)


def y_behind(values, lane, sublane):
    turned = pltpu.roll(values, 1, 1)
    return jnp.where(lane == 0, pltpu.roll(turned, 1, 0), turned)


def interface_flux(left, right, normal):
    rho_l, inv_l, vn_l, va_l, vb_l, mn_l, ma_l, mb_l, ba_l, bb_l = left
    rho_r, inv_r, vn_r, va_r, vb_r, mn_r, ma_r, mb_r, ba_r, bb_r = right
    normal_square = normal * normal
    square_l = ba_l * ba_l + bb_l * bb_l
    square_r = ba_r * ba_r + bb_r * bb_r
    arg_l = 1.0 + (normal_square + square_l) * inv_l
    arg_r = 1.0 + (normal_square + square_r) * inv_r
    signal_l = arg_l * lax.rsqrt(arg_l)
    signal_r = arg_r * lax.rsqrt(arg_r)
    lowest = jnp.minimum(jnp.minimum(vn_l - signal_l, vn_r - signal_r), 0.0)
    highest = jnp.maximum(jnp.maximum(vn_l + signal_l, vn_r + signal_r), 0.0)
    inverse = 1.0 / (highest - lowest)
    weight_l = highest * inverse
    weight_r = -lowest * inverse
    jump = lowest * weight_l

    def mix(flux_l, flux_r, cons_l, cons_r):
        return weight_l * flux_l + weight_r * flux_r + jump * (cons_r - cons_l)

    return (
        mix(mn_l, mn_r, rho_l, rho_r),
        mix(
            mn_l * vn_l + (rho_l + 0.5 * square_l),
            mn_r * vn_r + (rho_r + 0.5 * square_r),
            mn_l,
            mn_r,
        )
        - 0.5 * normal_square,
        mix(mn_l * va_l - normal * ba_l, mn_r * va_r - normal * ba_r, ma_l, ma_r),
        mix(mn_l * vb_l - normal * bb_l, mn_r * vb_r - normal * bb_r, mb_l, mb_r),
        mix(ba_l * vn_l - normal * va_l, ba_r * vn_r - normal * va_r, ba_l, ba_r),
        mix(bb_l * vn_l - normal * vb_l, bb_r * vn_r - normal * vb_r, bb_l, bb_r),
    )


def stage(count, source, base, base_skip, target, prim, fluxes, edges, lane):
    sublane = None
    ahead = lambda values: y_ahead(values, lane, sublane)
    behind = lambda values: y_behind(values, lane, sublane)

    def cells(row, carry):
        for z in range(2):
            rho = source[row, 0, z]
            inv = 1.0 / rho
            prim[row, 0, z] = inv
            prim[row, 1, z] = source[row, 1, z] * inv
            prim[row, 2, z] = source[row, 2, z] * inv
            prim[row, 3, z] = source[row, 3, z] * inv
            prim[row, 4, z] = 0.5 * (source[row, 4, z] + source[row - 1, 4, z])
            by = source[row, 5, z]
            prim[row, 5, z] = 0.5 * (by + behind(by))
            prim[row, 6, z] = 0.5 * (source[row, 6, z] + source[row, 6, 1 - z])
        return carry

    def side(row, z):
        rho = source[row, 0, z]
        momentum = [source[row, 1 + n, z] for n in range(3)]
        velocity = [prim[row, 1 + n, z] for n in range(3)]
        center = [prim[row, 4 + n, z] for n in range(3)]
        return rho, prim[row, 0, z], velocity, momentum, center

    def along(parts, n):
        rho, inv, velocity, momentum, center = parts
        a, b = (n + 1) % 3, (n + 2) % 3
        return (
            rho,
            inv,
            velocity[n],
            velocity[a],
            velocity[b],
            momentum[n],
            momentum[a],
            momentum[b],
            center[a],
            center[b],
        )

    def flux_x(row):
        for z in range(2):
            out = interface_flux(
                along(side(row, z), 0), along(side(row + 1, z), 0), source[row, 4, z]
            )
            for n in range(4):
                fluxes[row, n, z] = out[n]
            fluxes[row, 4, z] = out[4] + ahead(out[4])
            fluxes[row, 5, z] = out[5]

    def flux_y(row):
        for z in range(2):
            rho, inv, velocity, momentum, center = side(row, z)
            next_rho = ahead(rho)
            next_velocity = [ahead(v) for v in velocity]
            next_center = [ahead(center[0]), None, ahead(center[2])]
            shifted = (
                next_rho,
                1.0 / next_rho,
                next_velocity,
                [next_rho * v for v in next_velocity],
                next_center,
            )
            out = interface_flux(
                along((rho, inv, velocity, momentum, center), 1),
                along(shifted, 1),
                source[row, 5, z],
            )
            for n in range(4):
                fluxes[row, 6 + n, z] = out[n] - behind(out[n])
            fluxes[row, 10, z] = out[4]
            fluxes[row, 11, z] = out[5]

    def flux_z(row):
        for z in range(2):
            out = interface_flux(
                along(side(row, z), 2), along(side(row, 1 - z), 2), source[row, 6, z]
            )
            for n in range(4):
                fluxes[row, 12 + n, z] = out[n]
            fluxes[row, 16, z] = out[4]
            fluxes[row, 17, z] = out[5] + ahead(out[5])

    def inner(row, carry):
        flux_x(row)
        flux_y(row)
        flux_z(row)
        return carry

    def update(row, carry):
        edge_z, edge_x, edge_y = [], [], []
        for z in range(2):
            edge_z.append(
                0.25 * (fluxes[row, 11, z] + fluxes[row + 1, 11, z] - fluxes[row, 4, z])
            )
            edge_x.append(
                0.25 * (fluxes[row, 17, z] - fluxes[row, 10, z] - fluxes[row, 10, 1 - z])
            )
            edge_y.append(
                0.25
                * (
                    fluxes[row, 5, z]
                    + fluxes[row, 5, 1 - z]
                    - fluxes[row, 16, z]
                    - fluxes[row + 1, 16, z]
                )
            )
            edges[row, 0, z] = edge_z[z]
            edges[row, 1, z] = edge_y[z]

        def put(member, z, rate):
            value = source[row, member, z] + time_step * rate
            if base is not None:
                value = 0.5 * base[row + base_skip, member, z] + 0.5 * value
            target[row - 1, member, z] = value

        def diverge(z, nx, ny, nz):
            return (
                (fluxes[row, nx, z] - fluxes[row - 1, nx, z])
                + fluxes[row, 6 + ny, z]
                + (fluxes[row, 12 + nz, z] - fluxes[row, 12 + nz, 1 - z])
            )

        for z in range(2):
            put(0, z, -diverge(z, 0, 0, 0))
            put(1, z, 2.0 * rotation * source[row, 2, z] - diverge(z, 1, 3, 2))
            put(
                2,
                z,
                -diverge(z, 2, 1, 3) - (2.0 - shear_rate) * rotation * source[row, 1, z],
            )
            put(3, z, -diverge(z, 3, 2, 1))
            put(4, z, (edge_y[z] - edge_y[1 - z]) - (edge_z[z] - behind(edge_z[z])))
            put(5, z, (edge_z[z] - edges[row - 1, 0, z]) - (edge_x[z] - edge_x[1 - z]))
            put(6, z, (edge_x[z] - behind(edge_x[z])) - (edge_y[z] - edges[row - 1, 1, z]))
        return carry

    lax.fori_loop(1, count + 1, cells, 0)
    lax.fori_loop(1, count, inner, 0)
    flux_y(count)
    flux_z(count)
    lax.fori_loop(1, count, update, 0)


def rolled(twice, amount, lane):
    blocks = amount // LANES
    cells = amount % LANES
    here = pltpu.roll(twice[pl.ds(ROWS - blocks, ROWS), :], cells, 1)
    before = pltpu.roll(twice[pl.ds(ROWS - 1 - blocks, ROWS), :], cells, 1)
    return jnp.where(lane >= cells, here, before)


def advance_kernel(
    offsets, ghost_offsets, shear, place, received, send, state, first, prim, fluxes, edges, twice
):
    cycle = PARTS * LANES
    radial = place[0]
    own = place[1]
    radial_count = place[2]
    row_of = radial * ROWS + own
    total = radial_count * ROWS
    lane = lax.broadcasted_iota(jnp.int32, (ROWS, LANES), 1)

    def load(row, index):
        return received[pl.ds((row - 1) * SLABS + index, PARTS, stride=LANES), :]

    for z in range(2):
        state[0, 4, z] = received[pl.ds(126 + z, PARTS, stride=LANES), :]

    def fetch(row, carry):
        for index in range(SLABS):
            state[row, index // 2, index % 2] = load(row, index)
        return carry

    lax.fori_loop(1, FULL + 1, fetch, 0)

    def turn(ref, row, amount):
        for index in range(SLABS):
            values = ref[row, index // 2, index % 2]
            twice[index, 0:ROWS, :] = values
            twice[index, ROWS : 2 * ROWS, :] = values
        for index in range(SLABS):
            ref[row, index // 2, index % 2] = rolled(twice.at[index], amount, lane)

    def ghosts(row, carry):
        place_of = row_of - BELOW + row
        below = place_of < 0
        above = place_of >= total

        @pl.when(below | above)
        def _():
            shift = shear[0]
            turn(state, row, jnp.where(below, cycle - shift, shift) % cycle)

        return carry

    lax.fori_loop(0, FULL + 1, ghosts, 0)

    common = (prim, fluxes, edges, lane)
    stage(9, state, None, 0, first, *common)
    stage(7, first, state, 1, state, *common)

    def remap(row, carry):
        local = own - 3 + row
        below_offset = ghost_offsets[0, jnp.clip(local + ROWS, 0, ROWS - 1)]
        above_offset = ghost_offsets[2, jnp.clip(local - ROWS, 0, ROWS - 1)]
        own_offset = offsets[0, jnp.clip(local, 0, ROWS - 1)]
        offset = jnp.where(
            local < 0, below_offset, jnp.where(local >= ROWS, above_offset, own_offset)
        )
        place_of = row_of - 3 + row
        change = shear[1] - shear[0]
        amount = offset + jnp.where(
            place_of < 0, -change, jnp.where(place_of >= total, change, 0)
        )
        turn(state, row, (amount + 2 * cycle) % cycle)
        return carry

    lax.fori_loop(0, 6, remap, 0)

    stage(5, state, None, 0, first, *common)
    stage(3, first, state, 1, state, *common)

    turn(state, 1, offsets[1, own] % cycle)
    for index in range(SLABS):
        send[pl.ds(index, PARTS, stride=ROWS), :] = state[1, index // 2, index % 2]
    for index in range(SLABS, ROWS):
        send[pl.ds(index, PARTS, stride=ROWS), :] = jnp.zeros((PARTS, LANES), jnp.float32)


def unpack_kernel(received, density, momentum, field):
    for index in range(SLABS):
        rows = received[pl.ds(index, ROWS, stride=ROWS), :]
        member, level = divmod(index, 2)
        if member == 0:
            density[level] = rows
        elif member < 4:
            momentum[member - 1, level] = rows
        else:
            field[member - 4, level] = rows


def in_vmem(count):
    return [pl.BlockSpec(memory_space=pltpu.VMEM)] * count


def in_smem(count):
    return [pl.BlockSpec(memory_space=pltpu.SMEM)] * count


def f32(*shape):
    return jax.ShapeDtypeStruct(shape, jnp.float32)


params = pltpu.CompilerParams(vmem_limit_bytes=40 * 1024 * 1024)


def on_device(density, momentum, field, fargo_offsets, shear_shift):
    low, up = pl.pallas_call(
        strip_kernel,
        out_shape=(f32(LOW_ROWS, LANES), f32(UP_ROWS, LANES)),
        in_specs=in_vmem(4),
        out_specs=tuple(in_vmem(2)),
        compiler_params=params,
    )(density, momentum, field, fargo_offsets)
    count = lax.axis_size("gx")
    low = lax.ppermute(low, "gx", [(i, (i + 1) % count) for i in range(count)])
    up = lax.ppermute(up, "gx", [((i + 1) % count, i) for i in range(count)])
    send, ghost_offsets = pl.pallas_call(
        pack_kernel,
        out_shape=(f32(PARTS, LANES, LANES), jax.ShapeDtypeStruct((4, LANES), jnp.int32)),
        in_specs=in_vmem(5),
        out_specs=tuple(in_vmem(2)),
        scratch_shapes=[pltpu.VMEM((352, LANES), jnp.float32)],
        compiler_params=params,
    )(density, momentum, field, low, up)
    cycles = lax.all_to_all(send, "gy", split_axis=0, concat_axis=0, tiled=True)
    place = jnp.stack(
        [lax.axis_index("gx"), lax.axis_index("gy"), jnp.int32(count)]
    ).astype(jnp.int32)
    row = (2, ROWS, LANES)
    moved = pl.pallas_call(
        advance_kernel,
        out_shape=f32(PARTS * ROWS, LANES),
        in_specs=in_smem(4) + in_vmem(1),
        out_specs=in_vmem(1)[0],
        scratch_shapes=[
            pltpu.VMEM((FULL + 1, 7) + row, jnp.float32),
            pltpu.VMEM((FULL + 1, 7) + row, jnp.float32),
            pltpu.VMEM((FULL + 1, 7) + row, jnp.float32),
            pltpu.VMEM((FULL + 1, 18) + row, jnp.float32),
            pltpu.VMEM((FULL + 1, 2) + row, jnp.float32),
            pltpu.VMEM((SLABS, 2 * ROWS, LANES), jnp.float32),
        ],
        compiler_params=params,
    )(fargo_offsets, ghost_offsets, shear_shift, place, cycles.reshape(PARTS * LANES, LANES))
    moved = lax.all_to_all(
        moved.reshape(PARTS, ROWS, LANES), "gy", split_axis=0, concat_axis=0, tiled=True
    )
    return pl.pallas_call(
        unpack_kernel,
        out_shape=(f32(2, ROWS, LANES), f32(3, 2, ROWS, LANES), f32(3, 2, ROWS, LANES)),
        in_specs=in_vmem(1),
        out_specs=tuple(in_vmem(3)),
        compiler_params=params,
    )(moved.reshape(PARTS * ROWS, LANES))


def solution(mesh):
    placed = (
        P(None, "gx", "gy"),
        P(None, None, "gx", "gy"),
        P(None, None, "gx", "gy"),
        P(None, "gx"),
        P(),
    )
    return jax.shard_map(
        on_device,
        mesh=mesh,
        in_specs=placed,
        out_specs=(P(None, "gx", "gy"), P(None, None, "gx", "gy"), P(None, None, "gx", "gy")),
        check_vma=False,
    )
```

```python
import functools

import jax
import jax.numpy as jnp
from jax import lax
from jax.experimental import pallas as pl
from jax.experimental.pallas import tpu as pltpu
from jax.sharding import PartitionSpec as P

time_step = 0.03
rotation = 1.0
shear_rate = 1.5

ROWS = 16
LANES = 128
PARTS = 16
LEVELS = 2
SLABS = 14
BELOW = 5
ABOVE = 4
FULL = 9
LOW_ROWS = 72
UP_ROWS = 64


def strip_kernel(held, low, up):
    for index in range(SLABS):
        rows = held[index]
        low[pl.ds(index, BELOW, stride=SLABS), :] = rows[ROWS - BELOW :]
        up[pl.ds(index, ABOVE, stride=SLABS), :] = rows[:ABOVE]
    low[70:72, :] = held[SLABS, 0:2, :]
    up[56:58, :] = held[SLABS, 0:2, :]
    up[58:64, :] = jnp.zeros((6, LANES), jnp.float32)


def pack_kernel(held, low, up, send, ghost_offsets, rows_of):
    rows_of[0:70, :] = low[0:70, :]
    for index in range(SLABS):
        rows_of[pl.ds(BELOW * SLABS + index, ROWS, stride=SLABS), :] = held[index]
    rows_of[294:350, :] = up[0:56, :]
    for part in range(PARTS):
        start = SLABS * (part + 1)
        send[part, 0:126, :] = rows_of[start : start + 126, :]
        start = SLABS * part + 8
        send[part, 126:128, :] = rows_of[start : start + 2, :]
    ghost_offsets[0:2, :] = low[70:72, :].astype(jnp.int32)
    ghost_offsets[2:4, :] = up[56:58, :].astype(jnp.int32)


def y_ahead(values, lane):
    turned = pltpu.roll(values, LANES - 1, 1)
    return jnp.where(lane == LANES - 1, pltpu.roll(turned, ROWS - 1, 0), turned)


def y_behind(values, lane):
    turned = pltpu.roll(values, 1, 1)
    return jnp.where(lane == 0, pltpu.roll(turned, 1, 0), turned)


def interface_flux(left, right, normal, along):
    rho_l, inv_l, v_l, c_l = left
    rho_r, inv_r, v_r, c_r = right
    one, two = (along + 1) % 3, (along + 2) % 3
    normal_square = normal * normal
    square_l = c_l[one] * c_l[one] + c_l[two] * c_l[two]
    square_r = c_r[one] * c_r[one] + c_r[two] * c_r[two]
    arg_l = 1.0 + (normal_square + square_l) * inv_l
    arg_r = 1.0 + (normal_square + square_r) * inv_r
    signal_l = arg_l * lax.rsqrt(arg_l)
    signal_r = arg_r * lax.rsqrt(arg_r)
    lowest = jnp.minimum(jnp.minimum(v_l[along] - signal_l, v_r[along] - signal_r), 0.0)
    highest = jnp.maximum(jnp.maximum(v_l[along] + signal_l, v_r[along] + signal_r), 0.0)
    inverse = 1.0 / (highest - lowest)
    weight_l = highest * inverse
    weight_r = lowest * inverse
    jump = lowest * weight_l
    pull_l = weight_l * v_l[along] - jump
    pull_r = jump - weight_r * v_r[along]
    mass_l = rho_l * pull_l
    mass_r = rho_r * pull_r
    line_l = weight_l * normal
    line_r = weight_r * normal
    pressure = weight_l * (rho_l + 0.5 * square_l) - weight_r * (rho_r + 0.5 * square_r)

    def carried(n):
        return mass_l * v_l[n] + mass_r * v_r[n]

    return (
        mass_l + mass_r,
        carried(along) + (pressure - 0.5 * normal_square),
        carried(one) - (line_l * c_l[one] - line_r * c_r[one]),
        carried(two) - (line_l * c_l[two] - line_r * c_r[two]),
        (pull_l * c_l[one] + pull_r * c_r[one]) - (line_l * v_l[one] - line_r * v_r[one]),
        (pull_l * c_l[two] + pull_r * c_r[two]) - (line_l * v_l[two] - line_r * v_r[two]),
    )


FX, FX_BY, FX_BZ = 0, 8, 10
DY, FY_BZ, FY_BX = 11, 19, 20
DZ, FZ_BX, FZ_BY = 22, 26, 28
FLUXES = 30


def stage(count, source, base, target, prim, fluxes, edges, lane):
    ahead = lambda values: y_ahead(values, lane)
    behind = lambda values: y_behind(values, lane)

    def cells(row, carry):
        for z in range(2):
            inv = 1.0 / source[row, 0, z]
            prim[row, 0, z] = inv
            for n in range(3):
                prim[row, 1 + n, z] = source[row, 1 + n, z] * inv
            by = source[row, 5, z]
            prim[row, 4, z] = 0.5 * (source[row, 4, z] + source[row - 1, 4, z])
            prim[row, 5, z] = 0.5 * (by + behind(by))
        mean = 0.5 * (source[row, 6, 0] + source[row, 6, 1])
        prim[row, 6, 0] = mean
        return carry

    def states(row):
        mean = prim[row, 6, 0]
        return [
            (
                source[row, 0, z],
                prim[row, 0, z],
                [prim[row, 1 + n, z] for n in range(3)],
                [prim[row, 4, z], prim[row, 5, z], mean],
            )
            for z in range(2)
        ]

    def flux_x(row, here, there):
        total = None
        for z in range(2):
            out = interface_flux(here[z], there[z], source[row, 4, z], 0)
            for n in range(4):
                fluxes[row, FX + 2 * n + z] = out[n]
            fluxes[row, FX_BY + z] = out[4] + ahead(out[4])
            total = out[5] if z == 0 else total + out[5]
        fluxes[row, FX_BZ] = total

    def flux_y(row, here):
        total = None
        for z in range(2):
            rho, _, velocity, center = here[z]
            rho = ahead(rho)
            shifted = (
                rho,
                1.0 / rho,
                [ahead(v) for v in velocity],
                [ahead(center[0]), None, ahead(center[2])],
            )
            out = interface_flux(here[z], shifted, source[row, 5, z], 1)
            for n in range(4):
                fluxes[row, DY + 2 * n + z] = out[n] - behind(out[n])
            fluxes[row, FY_BX + z] = out[5]
            total = out[4] if z == 0 else total + out[4]
        fluxes[row, FY_BZ] = total

    def flux_z(row, here):
        first = None
        for z in range(2):
            out = interface_flux(here[z], here[1 - z], source[row, 6, z], 2)
            if z == 0:
                first = out
            else:
                for n in range(4):
                    fluxes[row, DZ + n] = first[n] - out[n]
            fluxes[row, FZ_BX + z] = out[4]
            fluxes[row, FZ_BY + z] = out[5] + ahead(out[5])

    def inner(row, carry):
        here = states(row)
        flux_y(row, here)
        flux_z(row, here)
        flux_x(row, here, states(row + 1))
        return carry

    def update(row, carry):
        edge_x, edge_y, edge_z, around = [], [], [], []
        for z in range(2):
            edge_z.append(
                (fluxes[row, FY_BX + z] + fluxes[row + 1, FY_BX + z]) - fluxes[row, FX_BY + z]
            )
            edge_x.append(fluxes[row, FZ_BY + z] - fluxes[row, FY_BZ])
            around.append(fluxes[row, FZ_BX + z] + fluxes[row + 1, FZ_BX + z])
            edge_y.append(fluxes[row, FX_BZ] - around[z])
            edges[row, 0, z] = edge_z[z]
            edges[row, 1, z] = edge_y[z]
        turn_x = around[1] - around[0]
        turn_y = fluxes[row, FZ_BY] - fluxes[row, FZ_BY + 1]

        def put(member, z, value):
            if base is not None:
                value = 0.5 * (base[row + 1, member, z] + value)
            target[row - 1, member, z] = value

        def diverge(z, nx, ny, nz):
            here = fluxes[row, FX + 2 * nx + z] - fluxes[row - 1, FX + 2 * nx + z]
            here = here + fluxes[row, DY + 2 * ny + z]
            return here + fluxes[row, DZ + nz] if z == 0 else here - fluxes[row, DZ + nz]

        quarter = 0.25 * time_step
        for z in range(2):
            rho, mx, my, mz = (source[row, n, z] for n in range(4))
            put(0, z, rho - time_step * diverge(z, 0, 0, 0))
            put(1, z, mx + time_step * (2.0 * rotation * my - diverge(z, 1, 3, 2)))
            put(
                2,
                z,
                my - time_step * (diverge(z, 2, 1, 3) + (2.0 - shear_rate) * rotation * mx),
            )
            put(3, z, mz - time_step * diverge(z, 3, 2, 1))
            change = edge_z[z] - behind(edge_z[z])
            change = turn_x - change if z == 0 else -turn_x - change
            put(4, z, source[row, 4, z] + quarter * change)
            change = edge_z[z] - edges[row - 1, 0, z]
            change = change - turn_y if z == 0 else change + turn_y
            put(5, z, source[row, 5, z] + quarter * change)
            change = (edge_x[z] - behind(edge_x[z])) - (edge_y[z] - edges[row - 1, 1, z])
            put(6, z, source[row, 6, z] + quarter * change)
        return carry

    lax.fori_loop(1, count + 1, cells, 0, unroll=True)
    lax.fori_loop(1, count, inner, 0, unroll=2)
    last = states(count)
    flux_y(count, last)
    flux_z(count, last)
    lax.fori_loop(1, count, update, 0, unroll=True)


def rolled(twice, amount, lane):
    blocks = amount // LANES
    cells = amount % LANES
    here = pltpu.roll(twice[pl.ds(ROWS - blocks, ROWS), :], cells, 1)
    before = pltpu.roll(twice[pl.ds(ROWS - 1 - blocks, ROWS), :], cells, 1)
    return jnp.where(lane >= cells, here, before)


def advance_kernel(
    scalars,
    ghost_offsets,
    received,
    send,
    state,
    first,
    prim,
    fluxes,
    edges,
    twice,
):
    cycle = PARTS * LANES
    radial = scalars[0]
    own = scalars[1]
    radial_count = scalars[2]
    row_of = radial * ROWS + own
    total = radial_count * ROWS
    lane = lax.broadcasted_iota(jnp.int32, (ROWS, LANES), 1)

    def load(row, index):
        return received[pl.ds((row - 1) * SLABS + index, PARTS, stride=LANES), :]

    for z in range(2):
        state[0, 4, z] = received[pl.ds(126 + z, PARTS, stride=LANES), :]

    def fetch(row, carry):
        for index in range(SLABS):
            state[row, index // 2, index % 2] = load(row, index)
        return carry

    lax.fori_loop(1, FULL + 1, fetch, 0)

    def turn(ref, row, amount):
        for index in range(SLABS):
            values = ref[row, index // 2, index % 2]
            twice[index, 0:ROWS, :] = values
            twice[index, ROWS : 2 * ROWS, :] = values
        for index in range(SLABS):
            ref[row, index // 2, index % 2] = rolled(twice.at[index], amount, lane)

    def ghosts(row, carry):
        place_of = row_of - BELOW + row
        below = place_of < 0
        above = place_of >= total

        @pl.when(below | above)
        def _():
            shift = scalars[3]
            turn(state, row, jnp.where(below, cycle - shift, shift) % cycle)

        return carry

    lax.fori_loop(0, FULL + 1, ghosts, 0)

    common = (prim, fluxes, edges, lane)
    stage(9, state, None, first, *common)
    stage(7, first, state, state, *common)

    def remap(row, carry):
        local = own - 3 + row
        below_offset = ghost_offsets[0, jnp.clip(local + ROWS, 0, ROWS - 1)]
        above_offset = ghost_offsets[2, jnp.clip(local - ROWS, 0, ROWS - 1)]
        own_offset = scalars[5 + jnp.clip(local, 0, ROWS - 1)]
        offset = jnp.where(
            local < 0, below_offset, jnp.where(local >= ROWS, above_offset, own_offset)
        )
        place_of = row_of - 3 + row
        change = scalars[4] - scalars[3]
        amount = offset + jnp.where(
            place_of < 0, -change, jnp.where(place_of >= total, change, 0)
        )
        turn(state, row, (amount + 2 * cycle) % cycle)
        return carry

    lax.fori_loop(0, 6, remap, 0, unroll=True)

    stage(5, state, None, first, *common)
    stage(3, first, state, state, *common)

    turn(state, 1, scalars[5 + ROWS + own] % cycle)
    for index in range(SLABS):
        send[pl.ds(index, PARTS, stride=ROWS), :] = state[1, index // 2, index % 2]
    for index in range(SLABS, ROWS):
        send[pl.ds(index, PARTS, stride=ROWS), :] = jnp.zeros((PARTS, LANES), jnp.float32)


def unpack_kernel(received, density, momentum, field):
    for index in range(SLABS):
        rows = received[pl.ds(index, ROWS, stride=ROWS), :]
        member, level = divmod(index, 2)
        if member == 0:
            density[level] = rows
        elif member < 4:
            momentum[member - 1, level] = rows
        else:
            field[member - 4, level] = rows


def in_vmem(count):
    return [pl.BlockSpec(memory_space=pltpu.VMEM)] * count


def in_smem(count):
    return [pl.BlockSpec(memory_space=pltpu.SMEM)] * count


def f32(*shape):
    return jax.ShapeDtypeStruct(shape, jnp.float32)


params = pltpu.CompilerParams(vmem_limit_bytes=16 * 1024 * 1024)


def scratch():
    row = (2, ROWS, LANES)
    return [
        pltpu.VMEM((FULL + 1, 7) + row, jnp.float32),
        pltpu.VMEM((FULL + 1, 7) + row, jnp.float32),
        pltpu.VMEM((FULL + 1, 7) + row, jnp.float32),
        pltpu.VMEM((FULL + 1, FLUXES, ROWS, LANES), jnp.float32),
        pltpu.VMEM((FULL + 1, 2) + row, jnp.float32),
        pltpu.VMEM((SLABS, 2 * ROWS, LANES), jnp.float32),
    ]


def on_device(density, momentum, field, fargo_offsets, shear_shift):
    shifts = jnp.pad(fargo_offsets, ((0, ROWS - LEVELS), (0, LANES - ROWS))).astype(jnp.float32)
    block = (-1, ROWS, LANES)
    held = jnp.concatenate(
        [density, momentum.reshape(block), field.reshape(block), shifts[None]], axis=0
    )
    low, up = pl.pallas_call(
        strip_kernel,
        out_shape=(f32(LOW_ROWS, LANES), f32(UP_ROWS, LANES)),
        in_specs=in_vmem(1),
        out_specs=tuple(in_vmem(2)),
        compiler_params=params,
    )(held)
    count = lax.axis_size("gx")
    low = lax.ppermute(low, "gx", [(i, (i + 1) % count) for i in range(count)])
    up = lax.ppermute(up, "gx", [((i + 1) % count, i) for i in range(count)])
    place = jnp.stack([lax.axis_index("gx"), lax.axis_index("gy"), jnp.int32(count)])
    scalars = jnp.concatenate(
        [place.astype(jnp.int32), shear_shift, fargo_offsets.reshape(LEVELS * ROWS)]
    )
    low, up, scalars = lax.optimization_barrier((low, up, scalars))
    send, ghost_offsets = pl.pallas_call(
        pack_kernel,
        out_shape=(f32(PARTS, LANES, LANES), jax.ShapeDtypeStruct((4, LANES), jnp.int32)),
        in_specs=in_vmem(3),
        out_specs=tuple(in_vmem(2)),
        scratch_shapes=[pltpu.VMEM((352, LANES), jnp.float32)],
        compiler_params=params,
    )(held, low, up)
    cycles = lax.all_to_all(send, "gy", split_axis=0, concat_axis=0, tiled=True)
    moved = pl.pallas_call(
        advance_kernel,
        out_shape=f32(PARTS * ROWS, LANES),
        in_specs=in_smem(2) + in_vmem(1),
        out_specs=in_vmem(1)[0],
        scratch_shapes=scratch(),
        compiler_params=params,
    )(scalars, ghost_offsets, cycles.reshape(PARTS * LANES, LANES))
    moved = lax.all_to_all(
        moved.reshape(PARTS, ROWS, LANES), "gy", split_axis=0, concat_axis=0, tiled=True
    )
    return pl.pallas_call(
        unpack_kernel,
        out_shape=(f32(2, ROWS, LANES), f32(3, 2, ROWS, LANES), f32(3, 2, ROWS, LANES)),
        in_specs=in_vmem(1),
        out_specs=tuple(in_vmem(3)),
        compiler_params=params,
    )(moved.reshape(PARTS * ROWS, LANES))


def solution(mesh):
    placed = (
        P(None, "gx", "gy"),
        P(None, None, "gx", "gy"),
        P(None, None, "gx", "gy"),
        P(None, "gx"),
        P(),
    )
    return jax.shard_map(
        on_device,
        mesh=mesh,
        in_specs=placed,
        out_specs=(P(None, "gx", "gy"), P(None, None, "gx", "gy"), P(None, None, "gx", "gy")),
        check_vma=False,
    )
```

```python
import functools

import jax
import jax.numpy as jnp
from jax import lax
from jax.experimental import pallas as pl
from jax.experimental.pallas import tpu as pltpu
from jax.sharding import PartitionSpec as P

time_step = 0.03
rotation = 1.0
shear_rate = 1.5

ROWS = 16
LANES = 128
PARTS = 16
HALF = PARTS // 2
LEVELS = 2
SLABS = 14
BELOW = 5
ABOVE = 4
FULL = 9
LOW_ROWS = 72
UP_ROWS = 64
CHUNK = 144


def strip_kernel(held, low, up):
    for index in range(SLABS):
        rows = held[index]
        low[pl.ds(index, BELOW, stride=SLABS), :] = rows[ROWS - BELOW :]
        up[pl.ds(index, ABOVE, stride=SLABS), :] = rows[:ABOVE]
    low[70:72, :] = held[SLABS, 0:2, :]
    up[56:58, :] = held[SLABS, 0:2, :]
    up[58:64, :] = jnp.zeros((6, LANES), jnp.float32)


def pack_kernel(held, low, up, send, ghost_offsets, rows_of):
    rows_of[0:70, :] = low[0:70, :]
    for index in range(SLABS):
        rows_of[pl.ds(BELOW * SLABS + index, ROWS, stride=SLABS), :] = held[index]
    rows_of[294:350, :] = up[0:56, :]
    for pair in range(HALF):
        start = SLABS * (2 * pair + 1)
        send[pair, 0:140, :] = rows_of[start : start + 140, :]
        start = SLABS * (2 * pair) + 8
        send[pair, 140:142, :] = rows_of[start : start + 2, :]
        send[pair, 142:CHUNK, :] = jnp.zeros((CHUNK - 142, LANES), jnp.float32)
    ghost_offsets[0:2, :] = low[70:72, :].astype(jnp.int32)
    ghost_offsets[2:4, :] = up[56:58, :].astype(jnp.int32)


def y_ahead(values, lane):
    turned = pltpu.roll(values, LANES - 1, 2)
    even, odd = turned[0], turned[1]
    last = lane == LANES - 1
    return jnp.stack(
        [jnp.where(last, odd, even), jnp.where(last, pltpu.roll(even, HALF - 1, 0), odd)]
    )


def y_behind(values, lane):
    turned = pltpu.roll(values, 1, 2)
    even, odd = turned[0], turned[1]
    first = lane == 0
    return jnp.stack([jnp.where(first, pltpu.roll(odd, 1, 0), even), jnp.where(first, even, odd)])


def interface_flux(left, right, normal, along):
    rho_l, inv_l, v_l, c_l = left
    rho_r, inv_r, v_r, c_r = right
    one, two = (along + 1) % 3, (along + 2) % 3
    normal_square = normal * normal
    square_l = c_l[one] * c_l[one] + c_l[two] * c_l[two]
    square_r = c_r[one] * c_r[one] + c_r[two] * c_r[two]
    arg_l = 1.0 + (normal_square + square_l) * inv_l
    arg_r = 1.0 + (normal_square + square_r) * inv_r
    signal_l = arg_l * lax.rsqrt(arg_l)
    signal_r = arg_r * lax.rsqrt(arg_r)
    lowest = jnp.minimum(jnp.minimum(v_l[along] - signal_l, v_r[along] - signal_r), 0.0)
    highest = jnp.maximum(jnp.maximum(v_l[along] + signal_l, v_r[along] + signal_r), 0.0)
    inverse = 1.0 / (highest - lowest)
    weight_l = highest * inverse
    weight_r = lowest * inverse
    jump = lowest * weight_l
    pull_l = weight_l * v_l[along] - jump
    pull_r = jump - weight_r * v_r[along]
    mass_l = rho_l * pull_l
    mass_r = rho_r * pull_r
    line_l = weight_l * normal
    line_r = weight_r * normal
    pressure = weight_l * (rho_l + 0.5 * square_l) - weight_r * (rho_r + 0.5 * square_r)

    def carried(n):
        return mass_l * v_l[n] + mass_r * v_r[n]

    return (
        mass_l + mass_r,
        carried(along) + (pressure - 0.5 * normal_square),
        carried(one) - (line_l * c_l[one] - line_r * c_r[one]),
        carried(two) - (line_l * c_l[two] - line_r * c_r[two]),
        (pull_l * c_l[one] + pull_r * c_r[one]) - (line_l * v_l[one] - line_r * v_r[one]),
        (pull_l * c_l[two] + pull_r * c_r[two]) - (line_l * v_l[two] - line_r * v_r[two]),
    )


FX, FX_BY, FX_BZ = 0, 8, 10
DY, FY_BZ, FY_BX = 11, 19, 20
DZ, FZ_BX, FZ_BY = 22, 26, 28
FLUXES = 30


def stage(count, source, base, target, prim, fluxes, edges, lane):
    ahead = lambda values: y_ahead(values, lane)
    behind = lambda values: y_behind(values, lane)

    def cells(row, carry):
        for z in range(2):
            inv = 1.0 / source[row, 0, z]
            prim[row, 0, z] = inv
            for n in range(3):
                prim[row, 1 + n, z] = source[row, 1 + n, z] * inv
            by = source[row, 5, z]
            prim[row, 4, z] = 0.5 * (source[row, 4, z] + source[row - 1, 4, z])
            prim[row, 5, z] = 0.5 * (by + behind(by))
        mean = 0.5 * (source[row, 6, 0] + source[row, 6, 1])
        prim[row, 6, 0] = mean
        return carry

    def states(row):
        mean = prim[row, 6, 0]
        return [
            (
                source[row, 0, z],
                prim[row, 0, z],
                [prim[row, 1 + n, z] for n in range(3)],
                [prim[row, 4, z], prim[row, 5, z], mean],
            )
            for z in range(2)
        ]

    def flux_x(row, here, there):
        total = None
        for z in range(2):
            out = interface_flux(here[z], there[z], source[row, 4, z], 0)
            for n in range(4):
                fluxes[row, FX + 2 * n + z] = out[n]
            fluxes[row, FX_BY + z] = out[4] + ahead(out[4])
            total = out[5] if z == 0 else total + out[5]
        fluxes[row, FX_BZ] = total

    def flux_y(row, here, radial_only):
        total = None
        for z in range(2):
            rho, _, velocity, center = here[z]
            rho = ahead(rho)
            shifted = (
                rho,
                1.0 / rho,
                [ahead(v) for v in velocity],
                [ahead(center[0]), None, ahead(center[2])],
            )
            out = interface_flux(here[z], shifted, source[row, 5, z], 1)
            fluxes[row, FY_BX + z] = out[5]
            if radial_only:
                continue
            for n in range(4):
                fluxes[row, DY + 2 * n + z] = out[n] - behind(out[n])
            total = out[4] if z == 0 else total + out[4]
        if not radial_only:
            fluxes[row, FY_BZ] = total

    def flux_z(row, here, radial_only):
        first = None
        for z in range(2):
            out = interface_flux(here[z], here[1 - z], source[row, 6, z], 2)
            fluxes[row, FZ_BX + z] = out[4]
            if radial_only:
                continue
            if z == 0:
                first = out
            else:
                for n in range(4):
                    fluxes[row, DZ + n] = first[n] - out[n]
            fluxes[row, FZ_BY + z] = out[5] + ahead(out[5])

    def two_rows(row, opening):
        one, two = states(row), states(row + 1)
        flux_y(row, one, opening)
        flux_z(row, one, opening)
        flux_x(row, one, two)
        three = states(row + 2)
        flux_y(row + 1, two, False)
        flux_z(row + 1, two, False)
        flux_x(row + 1, two, three)

    def update(row, radial_only):
        edge_x, edge_y, edge_z, around = [], [], [], []
        for z in range(2):
            edge_z.append(
                (fluxes[row, FY_BX + z] + fluxes[row + 1, FY_BX + z]) - fluxes[row, FX_BY + z]
            )
            around.append(fluxes[row, FZ_BX + z] + fluxes[row + 1, FZ_BX + z])
            edge_y.append(fluxes[row, FX_BZ] - around[z])
            edges[row, 0, z] = edge_z[z]
            edges[row, 1, z] = edge_y[z]
            if not radial_only:
                edge_x.append(fluxes[row, FZ_BY + z] - fluxes[row, FY_BZ])
        turn_x = around[1] - around[0]

        def put(member, z, value):
            if base is not None:
                value = 0.5 * (base[row + 1, member, z] + value)
            target[row - 1, member, z] = value

        def diverge(z, nx, ny, nz):
            here = fluxes[row, FX + 2 * nx + z] - fluxes[row - 1, FX + 2 * nx + z]
            here = here + fluxes[row, DY + 2 * ny + z]
            return here + fluxes[row, DZ + nz] if z == 0 else here - fluxes[row, DZ + nz]

        quarter = 0.25 * time_step
        for z in range(2):
            change = edge_z[z] - behind(edge_z[z])
            change = turn_x - change if z == 0 else -turn_x - change
            put(4, z, source[row, 4, z] + quarter * change)
        if radial_only:
            return
        turn_y = fluxes[row, FZ_BY] - fluxes[row, FZ_BY + 1]
        for z in range(2):
            rho, mx, my, mz = (source[row, n, z] for n in range(4))
            put(0, z, rho - time_step * diverge(z, 0, 0, 0))
            put(1, z, mx + time_step * (2.0 * rotation * my - diverge(z, 1, 3, 2)))
            put(
                2,
                z,
                my - time_step * (diverge(z, 2, 1, 3) + (2.0 - shear_rate) * rotation * mx),
            )
            put(3, z, mz - time_step * diverge(z, 3, 2, 1))
            change = edge_z[z] - edges[row - 1, 0, z]
            change = change - turn_y if z == 0 else change + turn_y
            put(5, z, source[row, 5, z] + quarter * change)
            change = (edge_x[z] - behind(edge_x[z])) - (edge_y[z] - edges[row - 1, 1, z])
            put(6, z, source[row, 6, z] + quarter * change)

    def more(pair, carry):
        two_rows(2 * pair + 1, False)
        return carry

    lax.fori_loop(1, count + 1, cells, 0, unroll=True)
    two_rows(1, True)
    lax.fori_loop(1, (count - 1) // 2, more, 0)
    last = states(count)
    flux_y(count, last, True)
    flux_z(count, last, True)
    for row in range(1, count):
        update(row, row == 1)


def rolled(twice, amount, lane):
    blocks = amount // LANES
    cells = amount % LANES
    parts = []
    for odd in range(2):
        start = PARTS - blocks + odd
        here = pltpu.roll(twice[pl.ds(start, HALF, stride=2), :], cells, 1)
        before = pltpu.roll(twice[pl.ds(start - 1, HALF, stride=2), :], cells, 1)
        parts.append(jnp.where(lane >= cells, here, before))
    return jnp.stack(parts)


def to_blocks(ref, start, stride, values):
    for odd in range(2):
        ref[pl.ds(start + odd * stride, HALF, stride=2 * stride), :] = values[odd]


def advance_kernel(
    scalars,
    ghost_offsets,
    mine,
    other,
    send,
    state,
    first,
    prim,
    fluxes,
    edges,
    twice,
):
    cycle = PARTS * LANES
    radial = scalars[0]
    own = scalars[1]
    radial_count = scalars[2]
    row_of = radial * ROWS + own
    total = radial_count * ROWS
    lane = lax.broadcasted_iota(jnp.int32, (HALF, LANES), 1)

    core = own % 2

    def fetch_slab(row, member, z, start):
        for parity, blocks in ((core, mine), (1 - core, other)):
            state[row, member, z, parity] = blocks[pl.ds(start, HALF, stride=CHUNK), :]

    for z in range(2):
        fetch_slab(0, 4, z, jnp.where(core == 0, 140, 8) + z)

    def fetch(row, carry):
        for index in range(SLABS):
            fetch_slab(row, index // 2, index % 2, (row - 1 + core) * SLABS + index)
        return carry

    lax.fori_loop(1, FULL + 1, fetch, 0)

    def turn(ref, row, amount, members=range(7)):
        slabs = [(member, z) for member in members for z in range(2)]
        for place, (member, z) in enumerate(slabs):
            values = ref[row, member, z]
            to_blocks(twice.at[place], 0, 1, values)
            to_blocks(twice.at[place], PARTS, 1, values)
        for place, (member, z) in enumerate(slabs):
            ref[row, member, z] = rolled(twice.at[place], amount, lane)

    def ghosts(row, carry):
        place_of = row_of - BELOW + row
        below = place_of < 0
        above = place_of >= total

        @pl.when(below | above)
        def _():
            shift = scalars[3]
            turn(state, row, jnp.where(below, cycle - shift, shift) % cycle)

        return carry

    lax.fori_loop(0, FULL + 1, ghosts, 0)

    common = (prim, fluxes, edges, lane)
    stage(9, state, None, first, *common)
    stage(7, first, state, state, *common)

    def remap(row):
        local = own - 3 + row
        below_offset = ghost_offsets[0, jnp.clip(local + ROWS, 0, ROWS - 1)]
        above_offset = ghost_offsets[2, jnp.clip(local - ROWS, 0, ROWS - 1)]
        own_offset = scalars[5 + jnp.clip(local, 0, ROWS - 1)]
        offset = jnp.where(
            local < 0, below_offset, jnp.where(local >= ROWS, above_offset, own_offset)
        )
        place_of = row_of - 3 + row
        change = scalars[4] - scalars[3]
        amount = offset + jnp.where(
            place_of < 0, -change, jnp.where(place_of >= total, change, 0)
        )
        turn(state, row, (amount + 2 * cycle) % cycle, range(4, 5) if row == 0 else range(7))

    for row in range(6):
        remap(row)

    stage(5, state, None, first, *common)
    stage(3, first, state, state, *common)

    turn(state, 1, scalars[5 + ROWS + own] % cycle)
    for index in range(SLABS):
        to_blocks(send, index, ROWS, state[1, index // 2, index % 2])
    for index in range(SLABS, ROWS):
        send[pl.ds(index, PARTS, stride=ROWS), :] = jnp.zeros((PARTS, LANES), jnp.float32)


def unpack_kernel(received, density, momentum, field):
    for index in range(SLABS):
        rows = received[pl.ds(index, ROWS, stride=ROWS), :]
        member, level = divmod(index, 2)
        if member == 0:
            density[level] = rows
        elif member < 4:
            momentum[member - 1, level] = rows
        else:
            field[member - 4, level] = rows


def in_vmem(count):
    return [pl.BlockSpec(memory_space=pltpu.VMEM)] * count


def in_smem(count):
    return [pl.BlockSpec(memory_space=pltpu.SMEM)] * count


def f32(*shape):
    return jax.ShapeDtypeStruct(shape, jnp.float32)


params = pltpu.CompilerParams(vmem_limit_bytes=16 * 1024 * 1024)


def scratch():
    row = (2, 2, HALF, LANES)
    return [
        pltpu.VMEM((FULL + 1, 7) + row, jnp.float32),
        pltpu.VMEM((FULL + 1, 7) + row, jnp.float32),
        pltpu.VMEM((FULL + 1, 7) + row, jnp.float32),
        pltpu.VMEM((FULL + 1, FLUXES, 2, HALF, LANES), jnp.float32),
        pltpu.VMEM((FULL + 1, 2) + row, jnp.float32),
        pltpu.VMEM((SLABS, 2 * ROWS, LANES), jnp.float32),
    ]


def on_device(density, momentum, field, fargo_offsets, shear_shift):
    shifts = jnp.pad(fargo_offsets, ((0, ROWS - LEVELS), (0, LANES - ROWS))).astype(jnp.float32)
    block = (-1, ROWS, LANES)
    held = jnp.concatenate(
        [density, momentum.reshape(block), field.reshape(block), shifts[None]], axis=0
    )
    low, up = pl.pallas_call(
        strip_kernel,
        out_shape=(f32(LOW_ROWS, LANES), f32(UP_ROWS, LANES)),
        in_specs=in_vmem(1),
        out_specs=tuple(in_vmem(2)),
        compiler_params=params,
    )(held)
    count = lax.axis_size("gx")
    low = lax.ppermute(low, "gx", [(i, (i + 1) % count) for i in range(count)])
    up = lax.ppermute(up, "gx", [((i + 1) % count, i) for i in range(count)])
    place = jnp.stack([lax.axis_index("gx"), lax.axis_index("gy"), jnp.int32(count)])
    scalars = jnp.concatenate(
        [place.astype(jnp.int32), shear_shift, fargo_offsets.reshape(LEVELS * ROWS)]
    )
    low, up, scalars = lax.optimization_barrier((low, up, scalars))
    send, ghost_offsets = pl.pallas_call(
        pack_kernel,
        out_shape=(f32(HALF, CHUNK, LANES), jax.ShapeDtypeStruct((4, LANES), jnp.int32)),
        in_specs=in_vmem(3),
        out_specs=tuple(in_vmem(2)),
        scratch_shapes=[pltpu.VMEM((352, LANES), jnp.float32)],
        compiler_params=params,
    )(held, low, up)
    alike = [list(range(core, PARTS, 2)) for core in range(2)]
    mine = lax.all_to_all(
        send, "gy", split_axis=0, concat_axis=0, tiled=True, axis_index_groups=alike
    )
    mine = mine.reshape(HALF * CHUNK, LANES)
    other = lax.ppermute(mine, "gy", [(i, i ^ 1) for i in range(PARTS)])
    moved = pl.pallas_call(
        advance_kernel,
        out_shape=f32(PARTS * ROWS, LANES),
        in_specs=in_smem(2) + in_vmem(2),
        out_specs=in_vmem(1)[0],
        scratch_shapes=scratch(),
        compiler_params=params,
    )(scalars, ghost_offsets, mine, other)
    moved = lax.all_to_all(
        moved.reshape(PARTS, ROWS, LANES), "gy", split_axis=0, concat_axis=0, tiled=True
    )
    return pl.pallas_call(
        unpack_kernel,
        out_shape=(f32(2, ROWS, LANES), f32(3, 2, ROWS, LANES), f32(3, 2, ROWS, LANES)),
        in_specs=in_vmem(1),
        out_specs=tuple(in_vmem(3)),
        compiler_params=params,
    )(moved.reshape(PARTS * ROWS, LANES))


def solution(mesh):
    placed = (
        P(None, "gx", "gy"),
        P(None, None, "gx", "gy"),
        P(None, None, "gx", "gy"),
        P(None, "gx"),
        P(),
    )
    return jax.shard_map(
        on_device,
        mesh=mesh,
        in_specs=placed,
        out_specs=(P(None, "gx", "gy"), P(None, None, "gx", "gy"), P(None, None, "gx", "gy")),
        check_vma=False,
    )
```

```python
import functools

import jax
import jax.numpy as jnp
from jax import lax
from jax.experimental import pallas as pl
from jax.experimental.pallas import tpu as pltpu
from jax.sharding import PartitionSpec as P

time_step = 0.03
rotation = 1.0
shear_rate = 1.5

ROWS = 16
LANES = 128
PARTS = 16
HALF = PARTS // 2
LEVELS = 2
SLABS = 14
BELOW = 5
ABOVE = 4
FULL = 9
LOW_ROWS = 72
UP_ROWS = 64
CHUNK = 144


def strip_kernel(held, offsets, low, up):
    for index in range(SLABS):
        rows = held[index]
        low[pl.ds(index, BELOW, stride=SLABS), :] = rows[ROWS - BELOW :]
        up[pl.ds(index, ABOVE, stride=SLABS), :] = rows[:ABOVE]
    shifts = offsets[...].astype(jnp.float32)
    low[70:72, :] = jnp.zeros((2, LANES), jnp.float32)
    up[56:64, :] = jnp.zeros((8, LANES), jnp.float32)
    low[70:72, 0:ROWS] = shifts
    up[56:58, 0:ROWS] = shifts


def pack_kernel(held, low, up, send, ghost_offsets, rows_of):
    rows_of[0:70, :] = low[0:70, :]
    for index in range(SLABS):
        rows_of[pl.ds(BELOW * SLABS + index, ROWS, stride=SLABS), :] = held[index]
    rows_of[294:350, :] = up[0:56, :]
    for pair in range(HALF):
        start = SLABS * (2 * pair + 1)
        send[pair, 0:140, :] = rows_of[start : start + 140, :]
        start = SLABS * (2 * pair) + 8
        send[pair, 140:142, :] = rows_of[start : start + 2, :]
        send[pair, 142:CHUNK, :] = jnp.zeros((CHUNK - 142, LANES), jnp.float32)
    ghost_offsets[0:2, :] = low[70:72, :].astype(jnp.int32)
    ghost_offsets[2:4, :] = up[56:58, :].astype(jnp.int32)


def y_ahead(values, lane):
    turned = pltpu.roll(values, LANES - 1, 2)
    even, odd = turned[0], turned[1]
    last = lane == LANES - 1
    return jnp.stack(
        [jnp.where(last, odd, even), jnp.where(last, pltpu.roll(even, HALF - 1, 0), odd)]
    )


def y_behind(values, lane):
    turned = pltpu.roll(values, 1, 2)
    even, odd = turned[0], turned[1]
    first = lane == 0
    return jnp.stack([jnp.where(first, pltpu.roll(odd, 1, 0), even), jnp.where(first, even, odd)])


def interface_flux(left, right, normal, along):
    rho_l, inv_l, v_l, c_l = left
    rho_r, inv_r, v_r, c_r = right
    one, two = (along + 1) % 3, (along + 2) % 3
    normal_square = normal * normal
    square_l = c_l[one] * c_l[one] + c_l[two] * c_l[two]
    square_r = c_r[one] * c_r[one] + c_r[two] * c_r[two]
    arg_l = 1.0 + (normal_square + square_l) * inv_l
    arg_r = 1.0 + (normal_square + square_r) * inv_r
    signal_l = arg_l * lax.rsqrt(arg_l)
    signal_r = arg_r * lax.rsqrt(arg_r)
    lowest = jnp.minimum(jnp.minimum(v_l[along] - signal_l, v_r[along] - signal_r), 0.0)
    highest = jnp.maximum(jnp.maximum(v_l[along] + signal_l, v_r[along] + signal_r), 0.0)
    inverse = 1.0 / (highest - lowest)
    weight_l = highest * inverse
    weight_r = lowest * inverse
    jump = lowest * weight_l
    pull_l = weight_l * v_l[along] - jump
    pull_r = jump - weight_r * v_r[along]
    mass_l = rho_l * pull_l
    mass_r = rho_r * pull_r
    line_l = weight_l * normal
    line_r = weight_r * normal
    pressure = weight_l * (rho_l + 0.5 * square_l) - weight_r * (rho_r + 0.5 * square_r)

    def carried(n):
        return mass_l * v_l[n] + mass_r * v_r[n]

    return (
        mass_l + mass_r,
        carried(along) + (pressure - 0.5 * normal_square),
        carried(one) - (line_l * c_l[one] - line_r * c_r[one]),
        carried(two) - (line_l * c_l[two] - line_r * c_r[two]),
        (pull_l * c_l[one] + pull_r * c_r[one]) - (line_l * v_l[one] - line_r * v_r[one]),
        (pull_l * c_l[two] + pull_r * c_r[two]) - (line_l * v_l[two] - line_r * v_r[two]),
    )


FX, FX_BY, FX_BZ = 0, 8, 10
DY, FY_BZ, FY_BX = 11, 19, 20
DZ, FZ_BX, FZ_BY = 22, 26, 28
FLUXES = 30


def stage(count, source, base, target, prim, fluxes, edges, lane):
    ahead = lambda values: y_ahead(values, lane)
    behind = lambda values: y_behind(values, lane)

    def cells(row, carry):
        for z in range(2):
            inv = 1.0 / source[row, 0, z]
            prim[row, 0, z] = inv
            for n in range(3):
                prim[row, 1 + n, z] = source[row, 1 + n, z] * inv
            by = source[row, 5, z]
            prim[row, 4, z] = 0.5 * (source[row, 4, z] + source[row - 1, 4, z])
            prim[row, 5, z] = 0.5 * (by + behind(by))
        mean = 0.5 * (source[row, 6, 0] + source[row, 6, 1])
        prim[row, 6, 0] = mean
        return carry

    def states(row):
        mean = prim[row, 6, 0]
        return [
            (
                source[row, 0, z],
                prim[row, 0, z],
                [prim[row, 1 + n, z] for n in range(3)],
                [prim[row, 4, z], prim[row, 5, z], mean],
            )
            for z in range(2)
        ]

    def flux_x(row, here, there):
        total = None
        for z in range(2):
            out = interface_flux(here[z], there[z], source[row, 4, z], 0)
            for n in range(4):
                fluxes[row, FX + 2 * n + z] = out[n]
            fluxes[row, FX_BY + z] = out[4] + ahead(out[4])
            total = out[5] if z == 0 else total + out[5]
        fluxes[row, FX_BZ] = total

    def flux_y(row, here, radial_only):
        total = None
        for z in range(2):
            rho, _, velocity, center = here[z]
            rho = ahead(rho)
            shifted = (
                rho,
                1.0 / rho,
                [ahead(v) for v in velocity],
                [ahead(center[0]), None, ahead(center[2])],
            )
            out = interface_flux(here[z], shifted, source[row, 5, z], 1)
            fluxes[row, FY_BX + z] = out[5]
            if radial_only:
                continue
            for n in range(4):
                fluxes[row, DY + 2 * n + z] = out[n] - behind(out[n])
            total = out[4] if z == 0 else total + out[4]
        if not radial_only:
            fluxes[row, FY_BZ] = total

    def flux_z(row, here, radial_only):
        first = None
        for z in range(2):
            out = interface_flux(here[z], here[1 - z], source[row, 6, z], 2)
            fluxes[row, FZ_BX + z] = out[4]
            if radial_only:
                continue
            if z == 0:
                first = out
            else:
                for n in range(4):
                    fluxes[row, DZ + n] = first[n] - out[n]
            fluxes[row, FZ_BY + z] = out[5] + ahead(out[5])

    def two_rows(row, opening):
        one, two = states(row), states(row + 1)
        flux_y(row, one, opening)
        flux_z(row, one, opening)
        flux_x(row, one, two)
        three = states(row + 2)
        flux_y(row + 1, two, False)
        flux_z(row + 1, two, False)
        flux_x(row + 1, two, three)

    def update(row, radial_only):
        edge_x, edge_y, edge_z, around = [], [], [], []
        for z in range(2):
            edge_z.append(
                (fluxes[row, FY_BX + z] + fluxes[row + 1, FY_BX + z]) - fluxes[row, FX_BY + z]
            )
            around.append(fluxes[row, FZ_BX + z] + fluxes[row + 1, FZ_BX + z])
            edge_y.append(fluxes[row, FX_BZ] - around[z])
            edges[row, 0, z] = edge_z[z]
            edges[row, 1, z] = edge_y[z]
            if not radial_only:
                edge_x.append(fluxes[row, FZ_BY + z] - fluxes[row, FY_BZ])
        turn_x = around[1] - around[0]

        def put(member, z, value):
            if base is not None:
                value = 0.5 * (base[row + 1, member, z] + value)
            target[row - 1, member, z] = value

        def diverge(z, nx, ny, nz):
            here = fluxes[row, FX + 2 * nx + z] - fluxes[row - 1, FX + 2 * nx + z]
            here = here + fluxes[row, DY + 2 * ny + z]
            return here + fluxes[row, DZ + nz] if z == 0 else here - fluxes[row, DZ + nz]

        quarter = 0.25 * time_step
        for z in range(2):
            change = edge_z[z] - behind(edge_z[z])
            change = turn_x - change if z == 0 else -turn_x - change
            put(4, z, source[row, 4, z] + quarter * change)
        if radial_only:
            return
        turn_y = fluxes[row, FZ_BY] - fluxes[row, FZ_BY + 1]
        for z in range(2):
            rho, mx, my, mz = (source[row, n, z] for n in range(4))
            put(0, z, rho - time_step * diverge(z, 0, 0, 0))
            put(1, z, mx + time_step * (2.0 * rotation * my - diverge(z, 1, 3, 2)))
            put(
                2,
                z,
                my - time_step * (diverge(z, 2, 1, 3) + (2.0 - shear_rate) * rotation * mx),
            )
            put(3, z, mz - time_step * diverge(z, 3, 2, 1))
            change = edge_z[z] - edges[row - 1, 0, z]
            change = change - turn_y if z == 0 else change + turn_y
            put(5, z, source[row, 5, z] + quarter * change)
            change = (edge_x[z] - behind(edge_x[z])) - (edge_y[z] - edges[row - 1, 1, z])
            put(6, z, source[row, 6, z] + quarter * change)

    def more(pair, carry):
        two_rows(2 * pair + 1, False)
        return carry

    lax.fori_loop(1, count + 1, cells, 0, unroll=True)
    two_rows(1, True)
    lax.fori_loop(1, (count - 1) // 2, more, 0)
    last = states(count)
    flux_y(count, last, True)
    flux_z(count, last, True)
    for row in range(1, count):
        update(row, row == 1)


def to_blocks(ref, start, stride, values):
    for odd in range(2):
        ref[pl.ds(start + odd * stride, HALF, stride=2 * stride), :] = values[odd]


def advance_kernel(
    scalars,
    ghost_offsets,
    mine,
    other,
    send,
    state,
    first,
    prim,
    fluxes,
    edges,
    twice,
):
    cycle = PARTS * LANES
    radial = scalars[0]
    own = scalars[1]
    radial_count = scalars[2]
    row_of = radial * ROWS + own
    total = radial_count * ROWS
    lane = lax.broadcasted_iota(jnp.int32, (HALF, LANES), 1)

    core = own % 2

    def fetch_slab(row, member, z, start):
        for parity, blocks in ((core, mine), (1 - core, other)):
            state[row, member, z, parity] = blocks[pl.ds(start, HALF, stride=CHUNK), :]

    for z in range(2):
        fetch_slab(0, 4, z, jnp.where(core == 0, 140, 8) + z)

    def fetch(row, carry):
        for index in range(SLABS):
            fetch_slab(row, index // 2, index % 2, (row - 1 + core) * SLABS + index)
        return carry

    lax.fori_loop(1, FULL + 1, fetch, 0)

    def turn(ref, row, amount, members=range(7)):
        blocks = amount // LANES
        cells = amount % LANES
        swap = blocks % 2
        here = lane >= cells
        slabs = [(member, z) for member in members for z in range(2)]
        for place, (member, z) in enumerate(slabs):
            for parity, values in ((0, ref[row, member, z, swap]), (1, ref[row, member, z, 1 - swap])):
                twice[place, parity, 0:HALF, :] = values
                twice[place, parity, HALF : 2 * HALF, :] = values
        for place, (member, z) in enumerate(slabs):
            even = twice[place, 0, pl.ds((2 * HALF - blocks) // 2, HALF), :]
            odd = twice[place, 1, pl.ds(HALF - blocks // 2, HALF), :]
            even, odd = pltpu.roll(even, cells, 1), pltpu.roll(odd, cells, 1)
            ref[row, member, z, 0] = jnp.where(here, even, pltpu.roll(odd, 1, 0))
            ref[row, member, z, 1] = jnp.where(here, odd, even)

    def ghosts(row, carry):
        place_of = row_of - BELOW + row
        below = place_of < 0
        above = place_of >= total

        @pl.when(below | above)
        def _():
            shift = scalars[3]
            turn(state, row, jnp.where(below, cycle - shift, shift) % cycle)

        return carry

    lax.fori_loop(0, FULL + 1, ghosts, 0)

    common = (prim, fluxes, edges, lane)
    stage(9, state, None, first, *common)
    stage(7, first, state, state, *common)

    def remap(row):
        local = own - 3 + row
        below_offset = ghost_offsets[0, jnp.clip(local + ROWS, 0, ROWS - 1)]
        above_offset = ghost_offsets[2, jnp.clip(local - ROWS, 0, ROWS - 1)]
        own_offset = scalars[5 + jnp.clip(local, 0, ROWS - 1)]
        offset = jnp.where(
            local < 0, below_offset, jnp.where(local >= ROWS, above_offset, own_offset)
        )
        place_of = row_of - 3 + row
        change = scalars[4] - scalars[3]
        amount = offset + jnp.where(
            place_of < 0, -change, jnp.where(place_of >= total, change, 0)
        )
        turn(state, row, (amount + 2 * cycle) % cycle, range(4, 5) if row == 0 else range(7))

    for row in range(6):
        remap(row)

    stage(5, state, None, first, *common)
    stage(3, first, state, state, *common)

    turn(state, 1, scalars[5 + ROWS + own] % cycle)
    for index in range(SLABS):
        to_blocks(send, index, ROWS, state[1, index // 2, index % 2])
    for index in range(SLABS, ROWS):
        send[pl.ds(index, PARTS, stride=ROWS), :] = jnp.zeros((PARTS, LANES), jnp.float32)


def unpack_kernel(received, density, momentum, field):
    for index in range(SLABS):
        rows = received[pl.ds(index, ROWS, stride=ROWS), :]
        member, level = divmod(index, 2)
        if member == 0:
            density[level] = rows
        elif member < 4:
            momentum[member - 1, level] = rows
        else:
            field[member - 4, level] = rows


def in_vmem(count):
    return [pl.BlockSpec(memory_space=pltpu.VMEM)] * count


def in_smem(count):
    return [pl.BlockSpec(memory_space=pltpu.SMEM)] * count


def f32(*shape):
    return jax.ShapeDtypeStruct(shape, jnp.float32)


params = pltpu.CompilerParams(vmem_limit_bytes=16 * 1024 * 1024)


def scratch():
    row = (2, 2, HALF, LANES)
    return [
        pltpu.VMEM((FULL + 1, 7) + row, jnp.float32),
        pltpu.VMEM((FULL + 1, 7) + row, jnp.float32),
        pltpu.VMEM((FULL + 1, 7) + row, jnp.float32),
        pltpu.VMEM((FULL + 1, FLUXES, 2, HALF, LANES), jnp.float32),
        pltpu.VMEM((FULL + 1, 2) + row, jnp.float32),
        pltpu.VMEM((SLABS, 2, 2 * HALF, LANES), jnp.float32),
    ]


def on_device(density, momentum, field, fargo_offsets, shear_shift):
    block = (-1, ROWS, LANES)
    held = jnp.concatenate([density, momentum.reshape(block), field.reshape(block)], axis=0)
    low, up = pl.pallas_call(
        strip_kernel,
        out_shape=(f32(LOW_ROWS, LANES), f32(UP_ROWS, LANES)),
        in_specs=in_vmem(2),
        out_specs=tuple(in_vmem(2)),
        compiler_params=params,
    )(held, fargo_offsets)
    count = lax.axis_size("gx")
    low = lax.ppermute(low, "gx", [(i, (i + 1) % count) for i in range(count)])
    up = lax.ppermute(up, "gx", [((i + 1) % count, i) for i in range(count)])
    place = jnp.stack([lax.axis_index("gx"), lax.axis_index("gy"), jnp.int32(count)])
    scalars = jnp.concatenate(
        [place.astype(jnp.int32), shear_shift, fargo_offsets.reshape(LEVELS * ROWS)]
    )
    low, up, scalars = lax.optimization_barrier((low, up, scalars))
    send, ghost_offsets = pl.pallas_call(
        pack_kernel,
        out_shape=(f32(HALF, CHUNK, LANES), jax.ShapeDtypeStruct((4, LANES), jnp.int32)),
        in_specs=in_vmem(3),
        out_specs=tuple(in_vmem(2)),
        scratch_shapes=[pltpu.VMEM((352, LANES), jnp.float32)],
        compiler_params=params,
    )(held, low, up)
    alike = [list(range(core, PARTS, 2)) for core in range(2)]
    mine = lax.all_to_all(
        send, "gy", split_axis=0, concat_axis=0, tiled=True, axis_index_groups=alike
    )
    mine = mine.reshape(HALF * CHUNK, LANES)
    other = lax.ppermute(mine, "gy", [(i, i ^ 1) for i in range(PARTS)])
    moved = pl.pallas_call(
        advance_kernel,
        out_shape=f32(PARTS * ROWS, LANES),
        in_specs=in_smem(2) + in_vmem(2),
        out_specs=in_vmem(1)[0],
        scratch_shapes=scratch(),
        compiler_params=params,
    )(scalars, ghost_offsets, mine, other)
    moved = lax.all_to_all(
        moved.reshape(PARTS, ROWS, LANES), "gy", split_axis=0, concat_axis=0, tiled=True
    )
    return pl.pallas_call(
        unpack_kernel,
        out_shape=(f32(2, ROWS, LANES), f32(3, 2, ROWS, LANES), f32(3, 2, ROWS, LANES)),
        in_specs=in_vmem(1),
        out_specs=tuple(in_vmem(3)),
        compiler_params=params,
    )(moved.reshape(PARTS * ROWS, LANES))


def solution(mesh):
    placed = (
        P(None, "gx", "gy"),
        P(None, None, "gx", "gy"),
        P(None, None, "gx", "gy"),
        P(None, "gx"),
        P(),
    )
    return jax.shard_map(
        on_device,
        mesh=mesh,
        in_specs=placed,
        out_specs=(P(None, "gx", "gy"), P(None, None, "gx", "gy"), P(None, None, "gx", "gy")),
        check_vma=False,
    )
```

```python
import functools

import jax
import jax.numpy as jnp
from jax import lax
from jax.experimental import pallas as pl
from jax.experimental.pallas import tpu as pltpu
from jax.sharding import PartitionSpec as P

time_step = 0.03
rotation = 1.0
shear_rate = 1.5

ROWS = 16
LANES = 128
PARTS = 16
HALF = PARTS // 2
LEVELS = 2
SLABS = 14
BELOW = 5
ABOVE = 4
FULL = 9
LOW_ROWS = 72
UP_ROWS = 64
CHUNK = 144


def strip_kernel(held, offsets, low, up):
    for index in range(SLABS):
        rows = held[index]
        low[pl.ds(index, BELOW, stride=SLABS), :] = rows[ROWS - BELOW :]
        up[pl.ds(index, ABOVE, stride=SLABS), :] = rows[:ABOVE]
    shifts = offsets[...].astype(jnp.float32)
    low[70:72, :] = jnp.zeros((2, LANES), jnp.float32)
    up[56:64, :] = jnp.zeros((8, LANES), jnp.float32)
    low[70:72, 0:ROWS] = shifts
    up[56:58, 0:ROWS] = shifts


def pack_kernel(held, low, up, send, ghost_offsets, rows_of):
    rows_of[0:70, :] = low[0:70, :]
    for index in range(SLABS):
        rows_of[pl.ds(BELOW * SLABS + index, ROWS, stride=SLABS), :] = held[index]
    rows_of[294:350, :] = up[0:56, :]
    for pair in range(HALF):
        start = SLABS * (2 * pair + 1)
        send[pair, 0:140, :] = rows_of[start : start + 140, :]
        start = SLABS * (2 * pair) + 8
        send[pair, 140:142, :] = rows_of[start : start + 2, :]
        send[pair, 142:CHUNK, :] = jnp.zeros((CHUNK - 142, LANES), jnp.float32)
    ghost_offsets[0:2, :] = low[70:72, :].astype(jnp.int32)
    ghost_offsets[2:4, :] = up[56:58, :].astype(jnp.int32)
    ghost_offsets[4:8, :] = jnp.zeros((4, LANES), jnp.int32)


def y_ahead(values, lane):
    turned = pltpu.roll(values, LANES - 1, 2)
    even, odd = turned[0], turned[1]
    last = lane == LANES - 1
    return jnp.stack(
        [jnp.where(last, odd, even), jnp.where(last, pltpu.roll(even, HALF - 1, 0), odd)]
    )


def y_behind(values, lane):
    turned = pltpu.roll(values, 1, 2)
    even, odd = turned[0], turned[1]
    first = lane == 0
    return jnp.stack([jnp.where(first, pltpu.roll(odd, 1, 0), even), jnp.where(first, even, odd)])


def interface_flux(left, right, normal, along):
    rho_l, inv_l, v_l, c_l = left
    rho_r, inv_r, v_r, c_r = right
    one, two = (along + 1) % 3, (along + 2) % 3
    normal_square = normal * normal
    square_l = c_l[one] * c_l[one] + c_l[two] * c_l[two]
    square_r = c_r[one] * c_r[one] + c_r[two] * c_r[two]
    arg_l = 1.0 + (normal_square + square_l) * inv_l
    arg_r = 1.0 + (normal_square + square_r) * inv_r
    signal_l = arg_l * lax.rsqrt(arg_l)
    signal_r = arg_r * lax.rsqrt(arg_r)
    lowest = jnp.minimum(jnp.minimum(v_l[along] - signal_l, v_r[along] - signal_r), 0.0)
    highest = jnp.maximum(jnp.maximum(v_l[along] + signal_l, v_r[along] + signal_r), 0.0)
    inverse = 1.0 / (highest - lowest)
    weight_l = highest * inverse
    weight_r = lowest * inverse
    jump = lowest * weight_l
    pull_l = weight_l * v_l[along] - jump
    pull_r = jump - weight_r * v_r[along]
    mass_l = rho_l * pull_l
    mass_r = rho_r * pull_r
    line_l = weight_l * normal
    line_r = weight_r * normal
    pressure = weight_l * (rho_l + 0.5 * square_l) - weight_r * (rho_r + 0.5 * square_r)

    def carried(n):
        return mass_l * v_l[n] + mass_r * v_r[n]

    return (
        mass_l + mass_r,
        carried(along) + (pressure - 0.5 * normal_square),
        carried(one) - (line_l * c_l[one] - line_r * c_r[one]),
        carried(two) - (line_l * c_l[two] - line_r * c_r[two]),
        (pull_l * c_l[one] + pull_r * c_r[one]) - (line_l * v_l[one] - line_r * v_r[one]),
        (pull_l * c_l[two] + pull_r * c_r[two]) - (line_l * v_l[two] - line_r * v_r[two]),
    )


FX, FX_BY, FX_BZ = 0, 8, 10
DY, FY_BZ, FY_BX = 11, 19, 20
DZ, FZ_BX, FZ_BY = 22, 26, 28
FLUXES = 30


def stage(count, source, base, target, prim, fluxes, edges, lane):
    ahead = lambda values: y_ahead(values, lane)
    behind = lambda values: y_behind(values, lane)

    def cells(row, carry):
        for z in range(2):
            inv = 1.0 / source[row, 0, z]
            prim[row, 0, z] = inv
            for n in range(3):
                prim[row, 1 + n, z] = source[row, 1 + n, z] * inv
            by = source[row, 5, z]
            prim[row, 4, z] = 0.5 * (source[row, 4, z] + source[row - 1, 4, z])
            prim[row, 5, z] = 0.5 * (by + behind(by))
        mean = 0.5 * (source[row, 6, 0] + source[row, 6, 1])
        prim[row, 6, 0] = mean
        return carry

    def states(row):
        mean = prim[row, 6, 0]
        return [
            (
                source[row, 0, z],
                prim[row, 0, z],
                [prim[row, 1 + n, z] for n in range(3)],
                [prim[row, 4, z], prim[row, 5, z], mean],
            )
            for z in range(2)
        ]

    def flux_x(row, here, there):
        total = None
        for z in range(2):
            out = interface_flux(here[z], there[z], source[row, 4, z], 0)
            for n in range(4):
                fluxes[row, FX + 2 * n + z] = out[n]
            fluxes[row, FX_BY + z] = out[4] + ahead(out[4])
            total = out[5] if z == 0 else total + out[5]
        fluxes[row, FX_BZ] = total

    def flux_y(row, here, radial_only):
        total = None
        for z in range(2):
            rho, _, velocity, center = here[z]
            rho = ahead(rho)
            shifted = (
                rho,
                1.0 / rho,
                [ahead(v) for v in velocity],
                [ahead(center[0]), None, ahead(center[2])],
            )
            out = interface_flux(here[z], shifted, source[row, 5, z], 1)
            fluxes[row, FY_BX + z] = out[5]
            if radial_only:
                continue
            for n in range(4):
                fluxes[row, DY + 2 * n + z] = out[n] - behind(out[n])
            total = out[4] if z == 0 else total + out[4]
        if not radial_only:
            fluxes[row, FY_BZ] = total

    def flux_z(row, here, radial_only):
        first = None
        for z in range(2):
            out = interface_flux(here[z], here[1 - z], source[row, 6, z], 2)
            fluxes[row, FZ_BX + z] = out[4]
            if radial_only:
                continue
            if z == 0:
                first = out
            else:
                for n in range(4):
                    fluxes[row, DZ + n] = first[n] - out[n]
            fluxes[row, FZ_BY + z] = out[5] + ahead(out[5])

    def two_rows(row, opening):
        one, two = states(row), states(row + 1)
        flux_y(row, one, opening)
        flux_z(row, one, opening)
        flux_x(row, one, two)
        three = states(row + 2)
        flux_y(row + 1, two, False)
        flux_z(row + 1, two, False)
        flux_x(row + 1, two, three)

    def update(row, radial_only):
        edge_x, edge_y, edge_z, around = [], [], [], []
        for z in range(2):
            edge_z.append(
                (fluxes[row, FY_BX + z] + fluxes[row + 1, FY_BX + z]) - fluxes[row, FX_BY + z]
            )
            around.append(fluxes[row, FZ_BX + z] + fluxes[row + 1, FZ_BX + z])
            edge_y.append(fluxes[row, FX_BZ] - around[z])
            edges[row, 0, z] = edge_z[z]
            edges[row, 1, z] = edge_y[z]
            if not radial_only:
                edge_x.append(fluxes[row, FZ_BY + z] - fluxes[row, FY_BZ])
        turn_x = around[1] - around[0]

        def put(member, z, value):
            if base is not None:
                value = 0.5 * (base[row + 1, member, z] + value)
            target[row - 1, member, z] = value

        def diverge(z, nx, ny, nz):
            here = fluxes[row, FX + 2 * nx + z] - fluxes[row - 1, FX + 2 * nx + z]
            here = here + fluxes[row, DY + 2 * ny + z]
            return here + fluxes[row, DZ + nz] if z == 0 else here - fluxes[row, DZ + nz]

        quarter = 0.25 * time_step
        for z in range(2):
            change = edge_z[z] - behind(edge_z[z])
            change = turn_x - change if z == 0 else -turn_x - change
            put(4, z, source[row, 4, z] + quarter * change)
        if radial_only:
            return
        turn_y = fluxes[row, FZ_BY] - fluxes[row, FZ_BY + 1]
        for z in range(2):
            rho, mx, my, mz = (source[row, n, z] for n in range(4))
            put(0, z, rho - time_step * diverge(z, 0, 0, 0))
            put(1, z, mx + time_step * (2.0 * rotation * my - diverge(z, 1, 3, 2)))
            put(
                2,
                z,
                my - time_step * (diverge(z, 2, 1, 3) + (2.0 - shear_rate) * rotation * mx),
            )
            put(3, z, mz - time_step * diverge(z, 3, 2, 1))
            change = edge_z[z] - edges[row - 1, 0, z]
            change = change - turn_y if z == 0 else change + turn_y
            put(5, z, source[row, 5, z] + quarter * change)
            change = (edge_x[z] - behind(edge_x[z])) - (edge_y[z] - edges[row - 1, 1, z])
            put(6, z, source[row, 6, z] + quarter * change)

    def more(pair, carry):
        two_rows(2 * pair + 1, False)
        return carry

    lax.fori_loop(1, count + 1, cells, 0, unroll=True)
    two_rows(1, True)
    lax.fori_loop(1, (count - 1) // 2, more, 0)
    last = states(count)
    flux_y(count, last, True)
    flux_z(count, last, True)
    for row in range(1, count):
        update(row, row == 1)


def to_blocks(ref, start, stride, values):
    for odd in range(2):
        ref[pl.ds(start + odd * stride, HALF, stride=2 * stride), :] = values[odd]


def advance_kernel(
    scalars_of,
    ghost_offsets_of,
    mine,
    other,
    send,
    state,
    first,
    prim,
    fluxes,
    edges,
    twice,
    scalars,
    ghost_offsets,
    arrived,
):
    copies = [
        pltpu.make_async_copy(scalars_of, scalars, arrived.at[0]),
        pltpu.make_async_copy(ghost_offsets_of, ghost_offsets, arrived.at[1]),
    ]
    for copy in copies:
        copy.start()
    cycle = PARTS * LANES
    radial = lax.axis_index("gx")
    own = lax.axis_index("gy")
    radial_count = lax.axis_size("gx")
    row_of = radial * ROWS + own
    total = radial_count * ROWS
    lane = lax.broadcasted_iota(jnp.int32, (HALF, LANES), 1)

    core = own % 2

    def fetch_slab(row, member, z, start):
        for parity, blocks in ((core, mine), (1 - core, other)):
            state[row, member, z, parity] = blocks[pl.ds(start, HALF, stride=CHUNK), :]

    for z in range(2):
        fetch_slab(0, 4, z, jnp.where(core == 0, 140, 8) + z)

    def fetch(row, carry):
        for index in range(SLABS):
            fetch_slab(row, index // 2, index % 2, (row - 1 + core) * SLABS + index)
        return carry

    lax.fori_loop(1, FULL + 1, fetch, 0)

    def turn(ref, row, amount, members=range(7)):
        blocks = amount // LANES
        cells = amount % LANES
        swap = blocks % 2
        here = lane >= cells
        slabs = [(member, z) for member in members for z in range(2)]
        for place, (member, z) in enumerate(slabs):
            for parity, values in ((0, ref[row, member, z, swap]), (1, ref[row, member, z, 1 - swap])):
                twice[place, parity, 0:HALF, :] = values
                twice[place, parity, HALF : 2 * HALF, :] = values
        for place, (member, z) in enumerate(slabs):
            even = twice[place, 0, pl.ds((2 * HALF - blocks) // 2, HALF), :]
            odd = twice[place, 1, pl.ds(HALF - blocks // 2, HALF), :]
            even, odd = pltpu.roll(even, cells, 1), pltpu.roll(odd, cells, 1)
            ref[row, member, z, 0] = jnp.where(here, even, pltpu.roll(odd, 1, 0))
            ref[row, member, z, 1] = jnp.where(here, odd, even)

    for copy in copies:
        copy.wait()

    def ghosts(row, members):
        place_of = row_of - BELOW + row
        below = place_of < 0
        above = place_of >= total

        @pl.when(below | above)
        def _():
            shift = scalars[3]
            turn(state, row, jnp.where(below, cycle - shift, shift) % cycle, members)

    def whole_ghosts(row, carry):
        ghosts(row, range(7))
        return carry

    ghosts(0, range(4, 5))
    lax.fori_loop(1, FULL + 1, whole_ghosts, 0)

    common = (prim, fluxes, edges, lane)
    stage(9, state, None, first, *common)
    stage(7, first, state, state, *common)

    def remap(row):
        local = own - 3 + row
        below_offset = ghost_offsets[0, jnp.clip(local + ROWS, 0, ROWS - 1)]
        above_offset = ghost_offsets[2, jnp.clip(local - ROWS, 0, ROWS - 1)]
        own_offset = scalars[5 + jnp.clip(local, 0, ROWS - 1)]
        offset = jnp.where(
            local < 0, below_offset, jnp.where(local >= ROWS, above_offset, own_offset)
        )
        place_of = row_of - 3 + row
        change = scalars[4] - scalars[3]
        amount = offset + jnp.where(
            place_of < 0, -change, jnp.where(place_of >= total, change, 0)
        )
        turn(state, row, (amount + 2 * cycle) % cycle, range(4, 5) if row == 0 else range(7))

    for row in range(6):
        remap(row)

    stage(5, state, None, first, *common)
    stage(3, first, state, state, *common)

    turn(state, 1, scalars[5 + ROWS + own] % cycle)
    for index in range(SLABS):
        to_blocks(send, index, ROWS, state[1, index // 2, index % 2])
    for index in range(SLABS, ROWS):
        send[pl.ds(index, PARTS, stride=ROWS), :] = jnp.zeros((PARTS, LANES), jnp.float32)


def unpack_kernel(received, density, momentum, field):
    for index in range(SLABS):
        rows = received[pl.ds(index, ROWS, stride=ROWS), :]
        member, level = divmod(index, 2)
        if member == 0:
            density[level] = rows
        elif member < 4:
            momentum[member - 1, level] = rows
        else:
            field[member - 4, level] = rows


def in_vmem(count):
    return [pl.BlockSpec(memory_space=pltpu.VMEM)] * count


def in_smem(count):
    return [pl.BlockSpec(memory_space=pltpu.SMEM)] * count


def f32(*shape):
    return jax.ShapeDtypeStruct(shape, jnp.float32)


params = pltpu.CompilerParams(vmem_limit_bytes=16 * 1024 * 1024)


def scratch():
    row = (2, 2, HALF, LANES)
    return [
        pltpu.VMEM((FULL + 1, 7) + row, jnp.float32),
        pltpu.VMEM((FULL + 1, 7) + row, jnp.float32),
        pltpu.VMEM((FULL + 1, 7) + row, jnp.float32),
        pltpu.VMEM((FULL + 1, FLUXES, 2, HALF, LANES), jnp.float32),
        pltpu.VMEM((FULL + 1, 2) + row, jnp.float32),
        pltpu.VMEM((SLABS, 2, 2 * HALF, LANES), jnp.float32),
        pltpu.SMEM((3 + LEVELS + LEVELS * ROWS,), jnp.int32),
        pltpu.SMEM((8, LANES), jnp.int32),
        pltpu.SemaphoreType.DMA((2,)),
    ]


def on_device(density, momentum, field, fargo_offsets, shear_shift):
    block = (-1, ROWS, LANES)
    held = jnp.concatenate([density, momentum.reshape(block), field.reshape(block)], axis=0)
    low, up = pl.pallas_call(
        strip_kernel,
        out_shape=(f32(LOW_ROWS, LANES), f32(UP_ROWS, LANES)),
        in_specs=in_vmem(2),
        out_specs=tuple(in_vmem(2)),
        compiler_params=params,
    )(held, fargo_offsets)
    count = lax.axis_size("gx")
    low = lax.ppermute(low, "gx", [(i, (i + 1) % count) for i in range(count)])
    up = lax.ppermute(up, "gx", [((i + 1) % count, i) for i in range(count)])
    place = jnp.stack([lax.axis_index("gx"), lax.axis_index("gy"), jnp.int32(count)])
    scalars = jnp.concatenate(
        [place.astype(jnp.int32), shear_shift, fargo_offsets.reshape(LEVELS * ROWS)]
    )
    low, up, scalars = lax.optimization_barrier((low, up, scalars))
    send, ghost_offsets = pl.pallas_call(
        pack_kernel,
        out_shape=(f32(HALF, CHUNK, LANES), jax.ShapeDtypeStruct((8, LANES), jnp.int32)),
        in_specs=in_vmem(3),
        out_specs=tuple(in_vmem(2)),
        scratch_shapes=[pltpu.VMEM((352, LANES), jnp.float32)],
        compiler_params=params,
    )(held, low, up)
    alike = [list(range(core, PARTS, 2)) for core in range(2)]
    mine = lax.all_to_all(
        send, "gy", split_axis=0, concat_axis=0, tiled=True, axis_index_groups=alike
    )
    mine = mine.reshape(HALF * CHUNK, LANES)
    other = lax.ppermute(mine, "gy", [(i, i ^ 1) for i in range(PARTS)])
    moved = pl.pallas_call(
        advance_kernel,
        out_shape=f32(PARTS * ROWS, LANES),
        in_specs=in_vmem(4),
        out_specs=in_vmem(1)[0],
        scratch_shapes=scratch(),
        compiler_params=params,
    )(scalars, ghost_offsets, mine, other)
    moved = lax.all_to_all(
        moved.reshape(PARTS, ROWS, LANES), "gy", split_axis=0, concat_axis=0, tiled=True
    )
    return pl.pallas_call(
        unpack_kernel,
        out_shape=(f32(2, ROWS, LANES), f32(3, 2, ROWS, LANES), f32(3, 2, ROWS, LANES)),
        in_specs=in_vmem(1),
        out_specs=tuple(in_vmem(3)),
        compiler_params=params,
    )(moved.reshape(PARTS * ROWS, LANES))


def solution(mesh):
    placed = (
        P(None, "gx", "gy"),
        P(None, None, "gx", "gy"),
        P(None, None, "gx", "gy"),
        P(None, "gx"),
        P(),
    )
    return jax.shard_map(
        on_device,
        mesh=mesh,
        in_specs=placed,
        out_specs=(P(None, "gx", "gy"), P(None, None, "gx", "gy"), P(None, None, "gx", "gy")),
        check_vma=False,
    )
```

```python
import functools

import jax
import jax.numpy as jnp
from jax import lax
from jax.experimental import pallas as pl
from jax.experimental.pallas import tpu as pltpu
from jax.sharding import PartitionSpec as P

time_step = 0.03
rotation = 1.0
shear_rate = 1.5

ROWS = 16
LANES = 128
PARTS = 16
HALF = PARTS // 2
LEVELS = 2
SLABS = 14
BELOW = 5
ABOVE = 4
FULL = 9
LOW_ROWS = 72
UP_ROWS = 64
CHUNK = 144


def strip_kernel(held, offsets, low, up):
    for index in range(SLABS):
        rows = held[index]
        low[pl.ds(index, BELOW, stride=SLABS), :] = rows[ROWS - BELOW :]
        up[pl.ds(index, ABOVE, stride=SLABS), :] = rows[:ABOVE]
    shifts = offsets[...].astype(jnp.float32)
    low[70:72, :] = jnp.zeros((2, LANES), jnp.float32)
    up[56:64, :] = jnp.zeros((8, LANES), jnp.float32)
    low[70:72, 0:ROWS] = shifts
    up[56:58, 0:ROWS] = shifts


def pack_kernel(held, low, up, send, ghost_offsets, rows_of):
    rows_of[0:70, :] = low[0:70, :]
    for index in range(SLABS):
        rows_of[pl.ds(BELOW * SLABS + index, ROWS, stride=SLABS), :] = held[index]
    rows_of[294:350, :] = up[0:56, :]
    for pair in range(HALF):
        start = SLABS * (2 * pair + 1)
        send[pair, 0:140, :] = rows_of[start : start + 140, :]
        start = SLABS * (2 * pair) + 8
        send[pair, 140:142, :] = rows_of[start : start + 2, :]
        send[pair, 142:CHUNK, :] = jnp.zeros((CHUNK - 142, LANES), jnp.float32)
    ghost_offsets[0:2, :] = low[70:72, :].astype(jnp.int32)
    ghost_offsets[2:4, :] = up[56:58, :].astype(jnp.int32)
    ghost_offsets[4:8, :] = jnp.zeros((4, LANES), jnp.int32)


def y_ahead(values, lane):
    turned = pltpu.roll(values, LANES - 1, 2)
    even, odd = turned[0], turned[1]
    last = lane == LANES - 1
    return jnp.stack(
        [jnp.where(last, odd, even), jnp.where(last, pltpu.roll(even, HALF - 1, 0), odd)]
    )


def y_behind(values, lane):
    turned = pltpu.roll(values, 1, 2)
    even, odd = turned[0], turned[1]
    first = lane == 0
    return jnp.stack([jnp.where(first, pltpu.roll(odd, 1, 0), even), jnp.where(first, even, odd)])


def interface_flux(left, right, normal, along):
    rho_l, inv_l, v_l, c_l = left
    rho_r, inv_r, v_r, c_r = right
    one, two = (along + 1) % 3, (along + 2) % 3
    normal_square = normal * normal
    square_l = c_l[one] * c_l[one] + c_l[two] * c_l[two]
    square_r = c_r[one] * c_r[one] + c_r[two] * c_r[two]
    arg_l = 1.0 + (normal_square + square_l) * inv_l
    arg_r = 1.0 + (normal_square + square_r) * inv_r
    signal_l = arg_l * lax.rsqrt(arg_l)
    signal_r = arg_r * lax.rsqrt(arg_r)
    lowest = jnp.minimum(jnp.minimum(v_l[along] - signal_l, v_r[along] - signal_r), 0.0)
    highest = jnp.maximum(jnp.maximum(v_l[along] + signal_l, v_r[along] + signal_r), 0.0)
    inverse = 1.0 / (highest - lowest)
    weight_l = highest * inverse
    weight_r = lowest * inverse
    jump = lowest * weight_l
    pull_l = weight_l * v_l[along] - jump
    pull_r = jump - weight_r * v_r[along]
    mass_l = rho_l * pull_l
    mass_r = rho_r * pull_r
    line_l = weight_l * normal
    line_r = weight_r * normal
    pressure = weight_l * (rho_l + 0.5 * square_l) - weight_r * (rho_r + 0.5 * square_r)

    def carried(n):
        return mass_l * v_l[n] + mass_r * v_r[n]

    return (
        mass_l + mass_r,
        carried(along) + (pressure - 0.5 * normal_square),
        carried(one) - (line_l * c_l[one] - line_r * c_r[one]),
        carried(two) - (line_l * c_l[two] - line_r * c_r[two]),
        (pull_l * c_l[one] + pull_r * c_r[one]) - (line_l * v_l[one] - line_r * v_r[one]),
        (pull_l * c_l[two] + pull_r * c_r[two]) - (line_l * v_l[two] - line_r * v_r[two]),
    )


FX, FX_BY, FX_BZ = 0, 8, 10
DY, FY_BZ, FY_BX = 11, 19, 20
DZ, FZ_BX, FZ_BY = 22, 26, 28
FLUXES = 30


def stage(count, source, base, target, prim, fluxes, edges, lane):
    ahead = lambda values: y_ahead(values, lane)
    behind = lambda values: y_behind(values, lane)

    def cells(row, carry):
        for z in range(2):
            inv = 1.0 / source[row, 0, z]
            prim[row, 0, z] = inv
            for n in range(3):
                prim[row, 1 + n, z] = source[row, 1 + n, z] * inv
            by = source[row, 5, z]
            prim[row, 4, z] = 0.5 * (source[row, 4, z] + source[row - 1, 4, z])
            prim[row, 5, z] = 0.5 * (by + behind(by))
        mean = 0.5 * (source[row, 6, 0] + source[row, 6, 1])
        prim[row, 6, 0] = mean
        return carry

    def states(row):
        mean = prim[row, 6, 0]
        return [
            (
                source[row, 0, z],
                prim[row, 0, z],
                [prim[row, 1 + n, z] for n in range(3)],
                [prim[row, 4, z], prim[row, 5, z], mean],
            )
            for z in range(2)
        ]

    def flux_x(row, here, there):
        total = None
        for z in range(2):
            out = interface_flux(here[z], there[z], source[row, 4, z], 0)
            for n in range(4):
                fluxes[row, FX + 2 * n + z] = out[n]
            fluxes[row, FX_BY + z] = out[4] + ahead(out[4])
            total = out[5] if z == 0 else total + out[5]
        fluxes[row, FX_BZ] = total

    def flux_y(row, here, radial_only):
        total = None
        for z in range(2):
            rho, _, velocity, center = here[z]
            rho = ahead(rho)
            shifted = (
                rho,
                1.0 / rho,
                [ahead(v) for v in velocity],
                [ahead(center[0]), None, ahead(center[2])],
            )
            out = interface_flux(here[z], shifted, source[row, 5, z], 1)
            fluxes[row, FY_BX + z] = out[5]
            if radial_only:
                continue
            for n in range(4):
                fluxes[row, DY + 2 * n + z] = out[n] - behind(out[n])
            total = out[4] if z == 0 else total + out[4]
        if not radial_only:
            fluxes[row, FY_BZ] = total

    def flux_z(row, here, radial_only):
        first = None
        for z in range(2):
            out = interface_flux(here[z], here[1 - z], source[row, 6, z], 2)
            fluxes[row, FZ_BX + z] = out[4]
            if radial_only:
                continue
            if z == 0:
                first = out
            else:
                for n in range(4):
                    fluxes[row, DZ + n] = first[n] - out[n]
            fluxes[row, FZ_BY + z] = out[5] + ahead(out[5])

    def two_rows(row, opening):
        one, two = states(row), states(row + 1)
        flux_y(row, one, opening)
        flux_z(row, one, opening)
        flux_x(row, one, two)
        three = states(row + 2)
        flux_y(row + 1, two, False)
        flux_z(row + 1, two, False)
        flux_x(row + 1, two, three)

    def update(row, radial_only):
        edge_x, edge_y, edge_z, around = [], [], [], []
        for z in range(2):
            edge_z.append(
                (fluxes[row, FY_BX + z] + fluxes[row + 1, FY_BX + z]) - fluxes[row, FX_BY + z]
            )
            around.append(fluxes[row, FZ_BX + z] + fluxes[row + 1, FZ_BX + z])
            edge_y.append(fluxes[row, FX_BZ] - around[z])
            edges[row, 0, z] = edge_z[z]
            edges[row, 1, z] = edge_y[z]
            if not radial_only:
                edge_x.append(fluxes[row, FZ_BY + z] - fluxes[row, FY_BZ])
        turn_x = around[1] - around[0]

        def put(member, z, value):
            if base is not None:
                value = 0.5 * (base[row + 1, member, z] + value)
            target[row - 1, member, z] = value

        def diverge(z, nx, ny, nz):
            here = fluxes[row, FX + 2 * nx + z] - fluxes[row - 1, FX + 2 * nx + z]
            here = here + fluxes[row, DY + 2 * ny + z]
            return here + fluxes[row, DZ + nz] if z == 0 else here - fluxes[row, DZ + nz]

        quarter = 0.25 * time_step
        for z in range(2):
            change = edge_z[z] - behind(edge_z[z])
            change = turn_x - change if z == 0 else -turn_x - change
            put(4, z, source[row, 4, z] + quarter * change)
        if radial_only:
            return
        turn_y = fluxes[row, FZ_BY] - fluxes[row, FZ_BY + 1]
        for z in range(2):
            rho, mx, my, mz = (source[row, n, z] for n in range(4))
            put(0, z, rho - time_step * diverge(z, 0, 0, 0))
            put(1, z, mx + time_step * (2.0 * rotation * my - diverge(z, 1, 3, 2)))
            put(
                2,
                z,
                my - time_step * (diverge(z, 2, 1, 3) + (2.0 - shear_rate) * rotation * mx),
            )
            put(3, z, mz - time_step * diverge(z, 3, 2, 1))
            change = edge_z[z] - edges[row - 1, 0, z]
            change = change - turn_y if z == 0 else change + turn_y
            put(5, z, source[row, 5, z] + quarter * change)
            change = (edge_x[z] - behind(edge_x[z])) - (edge_y[z] - edges[row - 1, 1, z])
            put(6, z, source[row, 6, z] + quarter * change)

    def more(pair, carry):
        two_rows(2 * pair + 1, False)
        return carry

    lax.fori_loop(1, count + 1, cells, 0, unroll=True)
    two_rows(1, True)
    lax.fori_loop(1, (count - 1) // 2, more, 0)
    last = states(count)
    flux_y(count, last, True)
    flux_z(count, last, True)
    for row in range(1, count):
        update(row, row == 1)


def to_blocks(ref, start, stride, values):
    for odd in range(2):
        ref[pl.ds(start + odd * stride, HALF, stride=2 * stride), :] = values[odd]


def advance_kernel(
    scalars_of,
    ghost_offsets_of,
    mine,
    other,
    send,
    state,
    first,
    prim,
    fluxes,
    edges,
    twice,
    scalars,
    ghost_offsets,
    arrived,
):
    copies = [
        pltpu.make_async_copy(scalars_of, scalars, arrived.at[0]),
        pltpu.make_async_copy(ghost_offsets_of, ghost_offsets, arrived.at[1]),
    ]
    for copy in copies:
        copy.start()
    cycle = PARTS * LANES
    radial = lax.axis_index("gx")
    own = lax.axis_index("gy")
    radial_count = lax.axis_size("gx")
    row_of = radial * ROWS + own
    total = radial_count * ROWS
    lane = lax.broadcasted_iota(jnp.int32, (HALF, LANES), 1)

    core = own % 2

    def fetch_slab(row, member, z, start):
        for parity, blocks in ((core, mine), (1 - core, other)):
            state[row, member, z, parity] = blocks[pl.ds(start, HALF, stride=CHUNK), :]

    for z in range(2):
        fetch_slab(0, 4, z, jnp.where(core == 0, 140, 8) + z)

    def fetch(row, carry):
        for index in range(SLABS):
            fetch_slab(row, index // 2, index % 2, (row - 1 + core) * SLABS + index)
        return carry

    lax.fori_loop(1, FULL + 1, fetch, 0)

    def turn(ref, turns):
        slabs = []
        for row, amount, members in turns:
            blocks = amount // LANES
            slabs += [(row, blocks, amount % LANES, m, z) for m in members for z in range(2)]
        for place, (row, blocks, cells, member, z) in enumerate(slabs):
            swap = blocks % 2
            for parity, values in ((0, ref[row, member, z, swap]), (1, ref[row, member, z, 1 - swap])):
                twice[place, parity, 0:HALF, :] = values
                twice[place, parity, HALF : 2 * HALF, :] = values
        for place, (row, blocks, cells, member, z) in enumerate(slabs):
            here = lane >= cells
            even = twice[place, 0, pl.ds((2 * HALF - blocks) // 2, HALF), :]
            odd = twice[place, 1, pl.ds(HALF - blocks // 2, HALF), :]
            even, odd = pltpu.roll(even, cells, 1), pltpu.roll(odd, cells, 1)
            ref[row, member, z, 0] = jnp.where(here, even, pltpu.roll(odd, 1, 0))
            ref[row, member, z, 1] = jnp.where(here, odd, even)

    whole, radial_only = range(7), range(4, 5)
    for copy in copies:
        copy.wait()
    shift = scalars[3]

    @pl.when(row_of < BELOW)
    def _():
        back = (cycle - shift) % cycle
        turn(
            state,
            [
                (row, jnp.where(row_of - BELOW + row < 0, back, 0), radial_only if row == 0 else whole)
                for row in range(BELOW)
            ],
        )

    @pl.when(row_of + ABOVE >= total)
    def _():
        turn(
            state,
            [
                (row, jnp.where(row_of - BELOW + row >= total, shift % cycle, 0), whole)
                for row in range(BELOW + 1, FULL + 1)
            ],
        )

    common = (prim, fluxes, edges, lane)
    stage(9, state, None, first, *common)
    stage(7, first, state, state, *common)

    def remap(row):
        local = own - 3 + row
        below_offset = ghost_offsets[0, jnp.clip(local + ROWS, 0, ROWS - 1)]
        above_offset = ghost_offsets[2, jnp.clip(local - ROWS, 0, ROWS - 1)]
        own_offset = scalars[5 + jnp.clip(local, 0, ROWS - 1)]
        offset = jnp.where(
            local < 0, below_offset, jnp.where(local >= ROWS, above_offset, own_offset)
        )
        place_of = row_of - 3 + row
        change = scalars[4] - scalars[3]
        amount = offset + jnp.where(
            place_of < 0, -change, jnp.where(place_of >= total, change, 0)
        )
        return row, (amount + 2 * cycle) % cycle, radial_only if row == 0 else whole

    turn(state, [remap(row) for row in range(6)])

    stage(5, state, None, first, *common)
    stage(3, first, state, state, *common)

    turn(state, [(1, scalars[5 + ROWS + own] % cycle, whole)])
    for index in range(SLABS):
        to_blocks(send, index, ROWS, state[1, index // 2, index % 2])
    for index in range(SLABS, ROWS):
        send[pl.ds(index, PARTS, stride=ROWS), :] = jnp.zeros((PARTS, LANES), jnp.float32)


def unpack_kernel(received, density, momentum, field):
    for index in range(SLABS):
        rows = received[pl.ds(index, ROWS, stride=ROWS), :]
        member, level = divmod(index, 2)
        if member == 0:
            density[level] = rows
        elif member < 4:
            momentum[member - 1, level] = rows
        else:
            field[member - 4, level] = rows


def in_vmem(count):
    return [pl.BlockSpec(memory_space=pltpu.VMEM)] * count


def in_smem(count):
    return [pl.BlockSpec(memory_space=pltpu.SMEM)] * count


def f32(*shape):
    return jax.ShapeDtypeStruct(shape, jnp.float32)


params = pltpu.CompilerParams(vmem_limit_bytes=16 * 1024 * 1024)


def scratch():
    row = (2, 2, HALF, LANES)
    return [
        pltpu.VMEM((FULL + 1, 7) + row, jnp.float32),
        pltpu.VMEM((FULL + 1, 7) + row, jnp.float32),
        pltpu.VMEM((FULL + 1, 7) + row, jnp.float32),
        pltpu.VMEM((FULL + 1, FLUXES, 2, HALF, LANES), jnp.float32),
        pltpu.VMEM((FULL + 1, 2) + row, jnp.float32),
        pltpu.VMEM((72, 2, 2 * HALF, LANES), jnp.float32),
        pltpu.SMEM((3 + LEVELS + LEVELS * ROWS,), jnp.int32),
        pltpu.SMEM((8, LANES), jnp.int32),
        pltpu.SemaphoreType.DMA((2,)),
    ]


def on_device(density, momentum, field, fargo_offsets, shear_shift):
    block = (-1, ROWS, LANES)
    held = jnp.concatenate([density, momentum.reshape(block), field.reshape(block)], axis=0)
    low, up = pl.pallas_call(
        strip_kernel,
        out_shape=(f32(LOW_ROWS, LANES), f32(UP_ROWS, LANES)),
        in_specs=in_vmem(2),
        out_specs=tuple(in_vmem(2)),
        compiler_params=params,
    )(held, fargo_offsets)
    count = lax.axis_size("gx")
    low = lax.ppermute(low, "gx", [(i, (i + 1) % count) for i in range(count)])
    up = lax.ppermute(up, "gx", [((i + 1) % count, i) for i in range(count)])
    place = jnp.stack([lax.axis_index("gx"), lax.axis_index("gy"), jnp.int32(count)])
    scalars = jnp.concatenate(
        [place.astype(jnp.int32), shear_shift, fargo_offsets.reshape(LEVELS * ROWS)]
    )
    low, up, scalars = lax.optimization_barrier((low, up, scalars))
    send, ghost_offsets = pl.pallas_call(
        pack_kernel,
        out_shape=(f32(HALF, CHUNK, LANES), jax.ShapeDtypeStruct((8, LANES), jnp.int32)),
        in_specs=in_vmem(3),
        out_specs=tuple(in_vmem(2)),
        scratch_shapes=[pltpu.VMEM((352, LANES), jnp.float32)],
        compiler_params=params,
    )(held, low, up)
    alike = [list(range(core, PARTS, 2)) for core in range(2)]
    mine = lax.all_to_all(
        send, "gy", split_axis=0, concat_axis=0, tiled=True, axis_index_groups=alike
    )
    mine = mine.reshape(HALF * CHUNK, LANES)
    other = lax.ppermute(mine, "gy", [(i, i ^ 1) for i in range(PARTS)])
    moved = pl.pallas_call(
        advance_kernel,
        out_shape=f32(PARTS * ROWS, LANES),
        in_specs=in_vmem(4),
        out_specs=in_vmem(1)[0],
        scratch_shapes=scratch(),
        compiler_params=params,
    )(scalars, ghost_offsets, mine, other)
    moved = lax.all_to_all(
        moved.reshape(PARTS, ROWS, LANES), "gy", split_axis=0, concat_axis=0, tiled=True
    )
    return pl.pallas_call(
        unpack_kernel,
        out_shape=(f32(2, ROWS, LANES), f32(3, 2, ROWS, LANES), f32(3, 2, ROWS, LANES)),
        in_specs=in_vmem(1),
        out_specs=tuple(in_vmem(3)),
        compiler_params=params,
    )(moved.reshape(PARTS * ROWS, LANES))


def solution(mesh):
    placed = (
        P(None, "gx", "gy"),
        P(None, None, "gx", "gy"),
        P(None, None, "gx", "gy"),
        P(None, "gx"),
        P(),
    )
    return jax.shard_map(
        on_device,
        mesh=mesh,
        in_specs=placed,
        out_specs=(P(None, "gx", "gy"), P(None, None, "gx", "gy"), P(None, None, "gx", "gy")),
        check_vma=False,
    )
```
